256 devices in a mesh: dom: 64 (over z, x, core), rep: 4 (over y).
Axes of the slice: x: 4, y: 4, z: 8, core: 2. Of those that a mesh axis runs over, the one named last changes fastest.
Arguments:
- feats: bfloat16 [65536, 768], P('dom'), may hold values from -6 to 6
- seed_rows: int32 [65536], P(('dom', 'rep')), may hold values from 0 to 1023
- edge_rows: int32 [256, 64, 64], P(('dom', 'rep')), may hold values from 0 to 1023
- edge_slots: int32 [256, 64, 64], P(('dom', 'rep')), may hold values from 0 to 32, as said below
- slot_seeds: int32 [256, 64, 32], P(('dom', 'rep')), may hold values from 0 to 256, as said below
- w_self: bfloat16 [768, 1024], replicated, may hold values from -0.21875 to 0.21875
- w_neigh: bfloat16 [768, 1024], replicated, may hold values from -0.21875 to 0.21875
- bias: float32 [1024], replicated, may hold values from -3 to 3
- cotangent: bfloat16 [65536, 1024], P(('dom', 'rep')), may hold values from -6 to 6
Outputs:
- hidden_out: bfloat16 [65536, 1024], P(('dom', 'rep'))
- self_grad: bfloat16 [65536, 768], P(('dom', 'rep'))
- feat_grads: bfloat16 [65536, 768], P(('dom', 'rep'))
- grad_self: float32 [768, 1024], replicated
- grad_neigh: float32 [768, 1024], replicated
- grad_bias: float32 [1024], replicated
The draws below stay inside these ranges and needn't reach their ends.
Inputs may be any that keep to these rules, and one draw needn't show every extreme that they name: `edge_slots`: the value 32 marks an unused edge entry. In each bucket (one device, one destination partition) every used slot is named by at least one entry and the used entries name only used slots. Each device has a bucket with all 64 entries used, naming all 32 slots. `slot_seeds`: the value 256 marks an unused slot. Slot p from source partition o at group d * 4 + r is used exactly when the edge entries of device o * 4 + r for destination d name it; the used slots from one source name distinct seeds.
All inputs are finite; a program needn't handle non-finite values.
Results may differ from the reference program's by a relative error of at most 0.007.
Values may be sent and summed in bfloat16 or wider, within the bound.
No kernel may reach another device: no remote copies, remote signals or barrier semaphores. Data moves between devices by JAX's collectives and lax.ppermute only.
A program may use at most 128 MiB of HBM per device.

```python
import jax
import jax.numpy as jnp
from jax import lax

F = 768
H = 1024
ROWS_DEV = 1024
SEED_DEV = 256
PCAP = 32
ECAP = 64
SEEDS = 65536
NODES = 65536
N_DOM = 64
N_REP = 4


def shuffled(key, shape, length):
    scores = jax.random.randint(key, shape + (length,), 0, 1 << 20) * length + jnp.arange(length, dtype=jnp.int32)
    return jnp.argsort(scores, axis=-1).astype(jnp.int32)


def sampled_plan(key):
    keys = jax.random.split(key, 8)
    pairs = (N_DOM, N_REP, N_DOM)
    favored = jax.random.randint(keys[0], (N_DOM, N_REP, 1), 0, N_DOM)
    is_full = jnp.arange(N_DOM, dtype=jnp.int32)[None, None, :] == favored
    used = jax.random.randint(keys[1], pairs, (2 * PCAP + 4) // 5, PCAP + 1)
    used = jnp.where(is_full, PCAP, used)
    floor_edges = jnp.maximum(used, (2 * ECAP + 4) // 5)
    edges = jax.random.randint(keys[2], pairs, floor_edges, ECAP + 1)
    edges = jnp.where(is_full, ECAP, edges)
    slot_order = shuffled(keys[3], pairs, PCAP)
    live = SEED_DEV - SEED_DEV // 16
    seed_order = shuffled(keys[4], (N_DOM, N_REP), SEED_DEV)
    picks = shuffled(keys[5], pairs, live)[..., :PCAP]
    dest_order = jnp.broadcast_to(jnp.transpose(seed_order, (1, 0, 2))[None], pairs + (SEED_DEV,))
    chosen = jnp.take_along_axis(dest_order, picks, axis=-1)
    position = jnp.arange(PCAP, dtype=jnp.int32)
    by_position = jnp.where(position < used[..., None], chosen, SEED_DEV)
    inverse = jnp.argsort(slot_order, axis=-1)
    seeds_by_slot = jnp.take_along_axis(by_position, inverse, axis=-1)
    entry = jnp.arange(ECAP, dtype=jnp.int32)
    extra = jax.random.randint(keys[6], pairs + (ECAP,), 0, used[..., None])
    order_index = jnp.where(entry < used[..., None], entry, extra)
    slot_of_entry = jnp.take_along_axis(slot_order, order_index, axis=-1)
    slot_of_entry = jnp.where(entry < edges[..., None], slot_of_entry, PCAP)
    mixing = shuffled(keys[7], pairs, ECAP)
    slot_of_entry = jnp.take_along_axis(slot_of_entry, mixing, axis=-1)
    return (slot_of_entry.astype(jnp.int32), seeds_by_slot.astype(jnp.int32))


def draw_edge_slots(key, part):
    slots, seeds = sampled_plan(key)
    return slots.reshape(N_DOM * N_REP, N_DOM, ECAP)


def draw_slot_seeds(key, part):
    slots, seeds = sampled_plan(key)
    return jnp.transpose(seeds, (2, 1, 0, 3)).reshape(N_DOM * N_REP, N_DOM, PCAP)


def set_ends(values, key, least, high):
    shape = values.shape
    spot = [jax.random.randint(jax.random.fold_in(key, axis), (), 0, shape[axis]) for axis in range(len(shape))]
    values = values.at[tuple(spot)].set(least)
    longest = shape.index(max(shape))
    spot[longest] = (spot[longest] + 1) % shape[longest]
    return values.at[tuple(spot)].set(high)


def block_scale(stream_key, extent, pieces, least, high):
    gain, own = 1.0, jax.random.fold_in(stream_key, 6)
    for dim, blocks in pieces:
        steps = jnp.exp(jax.random.uniform(jax.random.fold_in(own, dim), (blocks,), jnp.float32, least / len(pieces), high / len(pieces)))
        gain = gain * jnp.repeat(steps, extent[dim] // blocks).reshape([-1 if axis == dim else 1 for axis in range(len(extent))])
    return gain


def scatter_about(key, dims, width, limit, cuts=(), held_as=jnp.bfloat16):
    gain = block_scale(key, dims, cuts, -0.22, 0.18) if cuts else 1.0
    entries = jax.random.normal(key, dims, jnp.float32) * width * gain
    return jnp.minimum(jnp.maximum(entries, -limit), limit).astype(held_as)


def setup_inputs(seed: int = 0) -> dict:
    key_of = jax.random.split(jax.random.key(seed), 10)
    return {
        "feats": scatter_about(key_of[0], (NODES, F), 1.0, 6.0, ((0, 64),)),
        "seed_rows": set_ends(jax.random.randint(key_of[1], (SEEDS,), 0, ROWS_DEV), jax.random.fold_in(key_of[1], 1), 0, ROWS_DEV - 1).astype(jnp.int32),
        "edge_rows": set_ends(jax.random.randint(key_of[2], (N_DOM * N_REP, N_DOM, ECAP), 0, ROWS_DEV), jax.random.fold_in(key_of[2], 1), 0, ROWS_DEV - 1).astype(jnp.int32),
        "edge_slots": draw_edge_slots(jax.random.fold_in(key_of[9], 71), 0),
        "slot_seeds": draw_slot_seeds(jax.random.fold_in(key_of[9], 71), 0),
        "w_self": scatter_about(key_of[5], (F, H), F ** -0.5, 0.21875),
        "w_neigh": scatter_about(key_of[6], (F, H), F ** -0.5, 0.21875),
        "bias": scatter_about(key_of[7], (H,), 0.5, 3.0, (), jnp.float32),
        "cotangent": scatter_about(key_of[8], (SEEDS, H), 1.0, 6.0, ((0, 256),)),
    }


def bucket_sums(gathered_rows, slots):
    sums = jax.ops.segment_sum(gathered_rows.astype(jnp.float32), slots, num_segments=PCAP + 1)[:PCAP]
    counts = jax.ops.segment_sum(jnp.ones(slots.shape, jnp.int32), slots, num_segments=PCAP + 1)[:PCAP]
    return (sums.astype(jnp.bfloat16), counts)

def reference(feats, seed_rows, edge_rows, edge_slots, slot_seeds, w_self, w_neigh, bias, cotangent):
    groups = N_DOM * N_REP
    blocks = feats.reshape(N_DOM, ROWS_DEV, F)
    rows_four = edge_rows.reshape(N_DOM, N_REP, N_DOM, ECAP)
    slots_four = edge_slots.reshape(N_DOM, N_REP, N_DOM, ECAP)
    source_ids = jnp.arange(N_DOM, dtype=jnp.int32)

    def gather_dest(device):
        dest = device // N_REP
        replica = device % N_REP
        rows = rows_four[:, replica, dest, :]
        slots = slots_four[:, replica, dest, :]
        gathered = blocks[source_ids[:, None], rows]
        partial_value, counts = jax.vmap(bucket_sums)(gathered, slots)
        seeds = slot_seeds[device].reshape(-1)
        agg_sum = jax.ops.segment_sum(partial_value.reshape(-1, F).astype(jnp.float32), seeds, num_segments=SEED_DEV + 1)[:SEED_DEV]
        degree_count = jax.ops.segment_sum(counts.reshape(-1), seeds, num_segments=SEED_DEV + 1)[:SEED_DEV]
        return (agg_sum, degree_count)
    agg_sum, degree_count = lax.map(gather_dest, jnp.arange(groups, dtype=jnp.int32))
    degree = jnp.maximum(degree_count.astype(jnp.float32), 1.0).reshape(SEEDS, 1)
    aggregate = (agg_sum.reshape(SEEDS, F) / degree).astype(jnp.bfloat16)
    owner_of_seed = jnp.arange(SEEDS, dtype=jnp.int32) // (N_REP * SEED_DEV)
    self_rows = blocks[owner_of_seed, seed_rows]
    pre = jnp.dot(self_rows, w_self, preferred_element_type=jnp.float32)
    pre = pre + jnp.dot(aggregate, w_neigh, preferred_element_type=jnp.float32) + bias[None, :]
    hidden_out = jax.nn.gelu(pre).astype(jnp.bfloat16)
    _, pullback = jax.vjp(jax.nn.gelu, pre)
    delta = pullback(cotangent.astype(jnp.float32))[0].astype(jnp.bfloat16)
    scale = SEEDS ** (-0.5)
    grad_self = jnp.dot(self_rows.T, delta, preferred_element_type=jnp.float32) * scale
    grad_neigh = jnp.dot(aggregate.T, delta, preferred_element_type=jnp.float32) * scale
    grad_bias = lax.optimization_barrier(jnp.sum(delta.astype(jnp.float32), axis=0)) * scale
    self_grad = jnp.dot(delta, w_self.T, preferred_element_type=jnp.float32).astype(jnp.bfloat16)
    delta_neigh = (delta.astype(jnp.float32) / degree).astype(jnp.bfloat16)
    aggregate_grad = jnp.dot(delta_neigh, w_neigh.T, preferred_element_type=jnp.float32).astype(jnp.bfloat16)
    grad_table = jnp.concatenate([aggregate_grad.reshape(groups, SEED_DEV, F), jnp.zeros((groups, 1, F), aggregate_grad.dtype)], axis=1)
    seed_table = jnp.concatenate([slot_seeds, jnp.full((groups, N_DOM, 1), SEED_DEV, jnp.int32)], axis=2)

    def owner_grads(owner):

        def replica_part(replica):
            dest_groups = jnp.arange(N_DOM, dtype=jnp.int32) * N_REP + replica
            table = seed_table[dest_groups, owner, :]
            slots = slots_four[owner, replica]
            seed_of_entry = jnp.take_along_axis(table, slots, axis=1)
            values = grad_table[dest_groups[:, None], seed_of_entry].astype(jnp.float32)
            return jax.ops.segment_sum(values.reshape(-1, F), rows_four[owner, replica].reshape(-1), num_segments=ROWS_DEV)
        return lax.optimization_barrier(jnp.sum(jax.vmap(replica_part)(jnp.arange(N_REP, dtype=jnp.int32)), axis=0))
    feat_grads = lax.map(owner_grads, jnp.arange(N_DOM, dtype=jnp.int32)).reshape(NODES, F).astype(jnp.bfloat16)
    return (hidden_out, self_grad, feat_grads, grad_self, grad_neigh, grad_bias)
```

```python
import jax
import jax.numpy as jnp
import numpy as np
from jax import lax
from jax.experimental import pallas as pl
from jax.experimental.pallas import tpu as pltpu
from jax.sharding import Mesh, PartitionSpec as P

DOM = ("z", "x", "c")
NEAR = ("c", "rep")
FAR = ("z", "x")
bf16 = jnp.bfloat16
f32 = jnp.float32

GROUP = 4
STEP = 4


def contract_first(left, right):
    return lax.dot_general(
        left, right, (((0,), (0,)), ((), ())), preferred_element_type=f32
    )


def contract_last(left, right):
    return lax.dot_general(
        left, right, (((1,), (1,)), ((), ())), preferred_element_type=f32
    )


def exchange(value, axes):
    return lax.all_to_all(value, axes, split_axis=0, concat_axis=0, tiled=True)


def select_kernel(rows_ref, keys_ref, feats_ref, select_ref, partial_ref, count_ref):
    row_count = feats_ref.shape[0]
    entries = rows_ref.shape[2]
    slots = select_ref.shape[0] // STEP
    row_ids = lax.broadcasted_iota(jnp.int32, (row_count, entries), 0)
    slot_ids = lax.broadcasted_iota(jnp.int32, (slots, entries), 0)
    ones = jnp.ones((8, entries), bf16)
    for step in range(STEP):
        by_row = jnp.where(row_ids == rows_ref[step], 1.0, 0.0).astype(bf16)
        by_slot = jnp.where(slot_ids == keys_ref[step], 1.0, 0.0).astype(bf16)
        select_ref[step * slots : (step + 1) * slots, :] = contract_last(
            by_slot, by_row
        ).astype(bf16)
        count_ref[step] = contract_last(ones, by_slot)[0:1]
    partial_ref[...] = jnp.dot(
        select_ref[...], feats_ref[...], preferred_element_type=f32
    ).astype(bf16)


def select_and_sum(feats, edge_rows, edge_slots, slot_cap):
    dests, entry_cap = edge_rows.shape
    row_count, width = feats.shape
    groups = dests // GROUP
    entries = GROUP * entry_cap
    slots = GROUP * slot_cap
    offset = (jnp.arange(dests, dtype=jnp.int32) % GROUP * slot_cap)[:, None]
    keys = jnp.where(edge_slots < slot_cap, edge_slots + offset, -1)
    return pl.pallas_call(
        select_kernel,
        grid=(groups // STEP,),
        in_specs=[
            pl.BlockSpec((STEP, 1, entries), lambda i: (i, 0, 0)),
            pl.BlockSpec((STEP, 1, entries), lambda i: (i, 0, 0)),
            pl.BlockSpec((row_count, width), lambda i: (0, 0)),
        ],
        out_specs=[
            pl.BlockSpec((STEP * slots, row_count), lambda i: (i, 0)),
            pl.BlockSpec((STEP * slots, width), lambda i: (i, 0)),
            pl.BlockSpec((STEP, 1, slots), lambda i: (i, 0, 0)),
        ],
        out_shape=[
            jax.ShapeDtypeStruct((groups * slots, row_count), bf16),
            jax.ShapeDtypeStruct((groups * slots, width), bf16),
            jax.ShapeDtypeStruct((groups, 1, slots), f32),
        ],
        compiler_params=pltpu.CompilerParams(vmem_limit_bytes=40 * 1024 * 1024),
        cost_estimate=pl.CostEstimate(
            flops=2 * groups * slots * row_count * (width + entries),
            bytes_accessed=2 * (row_count * width + groups * slots * (row_count + width)),
            transcendentals=0,
        ),
    )(
        edge_rows.reshape(groups, 1, entries),
        keys.reshape(groups, 1, entries),
        feats,
    )


def reduce_everywhere(left, bias_column, delta):
    near = lax.axis_size(NEAR)
    far = lax.axis_size(FAR)
    seeds, depth = left.shape
    width = delta.shape[1]
    block = depth // near
    piece = block // far
    columns = jnp.concatenate(
        [
            left.reshape(seeds, near, block),
            jnp.broadcast_to(bias_column[:, None, :], (seeds, near, bias_column.shape[1])),
        ],
        axis=2,
    ).reshape(seeds, -1)
    terms = contract_first(columns, delta).astype(bf16).reshape(near, -1, width)
    summed = jnp.sum(exchange(terms, NEAR).astype(f32), axis=0)
    pieces = jnp.concatenate(
        [
            summed[:block].reshape(far, piece, width),
            jnp.broadcast_to(summed[None, block : block + 2], (far, 2, width)),
        ],
        axis=1,
    ).astype(bf16)
    total = jnp.sum(exchange(pieces, FAR).astype(f32), axis=0)
    bias_total = total[piece]
    spread = exchange(
        jnp.broadcast_to(total.astype(bf16)[None], (far,) + total.shape), FAR
    )
    own = spread[:, :piece].reshape(block, width)
    full = exchange(jnp.broadcast_to(own[None], (near, block, width)), NEAR)
    return full.reshape(depth, width), bias_total


def on_device(
    feats, seed_rows, edge_rows, edge_slots, slot_seeds, w_self, w_neigh, bias, cotangent
):
    edge_rows = edge_rows[0]
    edge_slots = edge_slots[0]
    slot_seeds = slot_seeds[0]
    sources, slot_cap = slot_seeds.shape
    seed_count = seed_rows.shape[0]
    row_count, width = feats.shape
    replicas = lax.axis_size("rep")
    select, partial_value, counts = select_and_sum(feats, edge_rows, edge_slots, slot_cap)
    arrived = exchange(partial_value.reshape(sources, slot_cap, width), DOM)
    arrived_counts = exchange(counts.astype(bf16).reshape(sources, 1, slot_cap), DOM)
    seed_onehot = (
        slot_seeds.reshape(-1)[:, None] == jnp.arange(seed_count, dtype=jnp.int32)[None, :]
    ).astype(bf16)
    agg_sum = contract_first(seed_onehot, arrived.reshape(-1, width))
    degree_raw = contract_first(seed_onehot, arrived_counts.reshape(-1, 1))
    degree = jnp.maximum(degree_raw, 1.0)
    aggregate = (agg_sum / degree).astype(bf16)
    self_rows = jnp.take(feats, seed_rows, axis=0)
    pre = jnp.dot(self_rows, w_self, preferred_element_type=f32)
    pre = pre + jnp.dot(aggregate, w_neigh, preferred_element_type=f32) + bias[None, :]
    hidden_out = jax.nn.gelu(pre).astype(bf16)
    _, pullback = jax.vjp(jax.nn.gelu, pre)
    delta = pullback(cotangent.astype(f32))[0].astype(bf16)
    delta_neigh = (delta.astype(f32) / degree).astype(bf16)
    aggregate_grad = contract_last(delta_neigh, w_neigh).astype(bf16)
    routed = jnp.dot(seed_onehot, aggregate_grad, preferred_element_type=f32).astype(bf16)
    slot_grad = exchange(routed.reshape(sources, slot_cap, width), DOM)
    scale = float(seed_count * lax.axis_size(DOM) * replicas) ** (-0.5)
    marker = jnp.broadcast_to(
        (jnp.arange(16) == 0).astype(bf16)[None, :], (seed_count, 16)
    )
    grads, bias_total = reduce_everywhere(
        jnp.concatenate([self_rows, aggregate], axis=1), marker, delta
    )
    grads = grads.astype(f32) * scale
    self_grad = contract_last(delta, w_self).astype(bf16)
    local_sum = contract_first(select, slot_grad.reshape(-1, width)).astype(bf16)
    shares = exchange(local_sum.reshape(replicas, row_count // replicas, width), "rep")
    feat_grads = jnp.sum(shares.astype(f32), axis=0).astype(bf16)
    return (
        hidden_out,
        self_grad,
        feat_grads,
        grads[:width],
        grads[width:],
        bias_total * scale,
    )


def solution(mesh):
    fine = Mesh(
        np.asarray(mesh.devices).reshape(8, 4, 2, 4), ("z", "x", "c", "rep")
    )
    every = DOM + ("rep",)
    in_specs = (
        P(DOM, None),
        P(every),
        P(every, None, None),
        P(every, None, None),
        P(every, None, None),
        P(),
        P(),
        P(),
        P(every, None),
    )
    out_specs = (P(every, None), P(every, None), P(every, None), P(), P(), P())
    return jax.shard_map(
        on_device, mesh=fine, in_specs=in_specs, out_specs=out_specs, check_vma=False
    )
```

```python
import jax
import jax.numpy as jnp
import numpy as np
from jax import lax
from jax.experimental import pallas as pl
from jax.experimental.pallas import tpu as pltpu
from jax.sharding import Mesh, PartitionSpec as P

DOM = ("z", "x", "c")
NEAR = ("c", "rep")
FAR = ("z", "x")
bf16 = jnp.bfloat16
f32 = jnp.float32

GROUP = 4
STEP = 4
SPLIT = 4
EXTRA = 128
FIRST = 384
VMEM = pltpu.CompilerParams(vmem_limit_bytes=48 * 1024 * 1024)
MARGIN = 16


def contract_first(left, right):
    return lax.dot_general(
        left, right, (((0,), (0,)), ((), ())), preferred_element_type=f32
    )


def contract_last(left, right):
    return lax.dot_general(
        left, right, (((1,), (1,)), ((), ())), preferred_element_type=f32
    )


def exchange(value, axes):
    return lax.all_to_all(value, axes, split_axis=0, concat_axis=0, tiled=True)


def cost(flops, bytes_accessed):
    return pl.CostEstimate(flops=flops, bytes_accessed=bytes_accessed, transcendentals=0)


def select_kernel(rows_ref, keys_ref, feats_ref, select_ref, partial_ref):
    row_count, width = feats_ref.shape
    entries = rows_ref.shape[2]
    part = select_ref.shape[1] // STEP
    slots = SPLIT * part
    row_ids = lax.broadcasted_iota(jnp.int32, (row_count, entries), 0)
    slot_ids = lax.broadcasted_iota(jnp.int32, (slots, entries), 0)
    lanes = lax.broadcasted_iota(jnp.int32, (part, EXTRA), 1)
    for step in range(STEP):
        here = slice(step * part, (step + 1) * part)
        by_row = jnp.where(row_ids == rows_ref[step], 1.0, 0.0).astype(bf16)
        hits = jnp.where(slot_ids == keys_ref[step], 1.0, 0.0)
        chosen = contract_last(hits.astype(bf16), by_row).astype(bf16)
        count = jnp.sum(hits, axis=1, keepdims=True)
        tail = jnp.zeros((part, EXTRA), f32)
        for j in range(SPLIT):
            select_ref[j, here, :] = chosen[j * part : (j + 1) * part]
            tail = jnp.where(lanes == j, count[j * part : (j + 1) * part], tail)
        partial_ref[here, SPLIT * width :] = tail.astype(bf16)
    for j in range(SPLIT):
        partial_ref[:, j * width : (j + 1) * width] = jnp.dot(
            select_ref[j], feats_ref[...], preferred_element_type=f32
        ).astype(bf16)


def select_and_sum(feats, edge_rows, edge_slots, slot_cap):
    dests, entry_cap = edge_rows.shape
    row_count, width = feats.shape
    groups = dests // GROUP
    entries = GROUP * entry_cap
    s_count = slot_cap // SPLIT
    part = GROUP * s_count
    wide = SPLIT * width + EXTRA
    place = (jnp.arange(dests, dtype=jnp.int32) % GROUP * s_count)[:, None]
    keys = edge_slots // s_count * part + place + edge_slots % s_count
    keys = jnp.where(edge_slots < slot_cap, keys, -1)
    return pl.pallas_call(
        select_kernel,
        grid=(groups // STEP,),
        in_specs=[
            pl.BlockSpec((STEP, 1, entries), lambda i: (i, 0, 0)),
            pl.BlockSpec((STEP, 1, entries), lambda i: (i, 0, 0)),
            pl.BlockSpec((row_count, width), lambda i: (0, 0)),
        ],
        out_specs=[
            pl.BlockSpec((SPLIT, STEP * part, row_count), lambda i: (0, i, 0)),
            pl.BlockSpec((STEP * part, wide), lambda i: (i, 0)),
        ],
        out_shape=[
            jax.ShapeDtypeStruct((SPLIT, groups * part, row_count), bf16),
            jax.ShapeDtypeStruct((groups * part, wide), bf16),
        ],
        compiler_params=VMEM,
        cost_estimate=cost(
            2 * SPLIT * groups * part * row_count * (width + entries),
            2 * (row_count * width + groups * part * (SPLIT * row_count + wide)),
        ),
    )(
        edge_rows.reshape(groups, 1, entries),
        keys.reshape(groups, 1, entries),
        feats,
    )


def middle_kernel(
    arrived_ref,
    seeds_ref,
    base_ref,
    w_neigh_ref,
    cotangent_ref,
    hidden_ref,
    delta_ref,
    aggregate_ref,
    first_ref,
    second_ref,
    pre_ref,
    neigh_ref,
    degree_ref,
):
    seed_count = base_ref.shape[0]
    width = w_neigh_ref.shape[0]
    sent = seeds_ref.shape[2]
    ids = lax.broadcasted_iota(jnp.int32, (seed_count, sent), 0)
    lanes = lax.broadcasted_iota(jnp.int32, (seed_count, EXTRA), 1)

    def routing(j):
        return jnp.where(ids == seeds_ref[j], 1.0, 0.0).astype(bf16)

    total = jnp.zeros((seed_count, width), f32)
    counts = jnp.zeros((seed_count, EXTRA), f32)
    for j in range(SPLIT):
        route = routing(j)
        total += jnp.dot(
            route, arrived_ref[:, j * width : (j + 1) * width], preferred_element_type=f32
        )
        found = jnp.dot(route, arrived_ref[:, SPLIT * width :], preferred_element_type=f32)
        counts += jnp.where(lanes == j, found, 0.0)
    degree = jnp.maximum(jnp.sum(counts, axis=1, keepdims=True), 1.0)
    degree_ref[...] = jnp.broadcast_to(degree, (seed_count, EXTRA))
    aggregate_ref[...] = (total / degree).astype(bf16)
    pre_ref[...] = base_ref[...] + jnp.dot(
        aggregate_ref[...], w_neigh_ref[...], preferred_element_type=f32
    )

    rows = 16
    slope = (2.0 / np.pi) ** 0.5

    @pl.loop(0, seed_count // rows)
    def _(i):
        here = pl.ds(pl.multiple_of(i * rows, rows), rows)
        pre = pre_ref[here, :]
        square = pre * pre
        bend = jnp.tanh(slope * pre * (1.0 + 0.044715 * square))
        half = 0.5 * (1.0 + bend)
        hidden_ref[here, :] = (pre * half).astype(bf16)
        steep = half + 0.5 * pre * (1.0 - bend * bend) * (
            slope * (1.0 + 3 * 0.044715 * square)
        )
        delta = (cotangent_ref[here, :].astype(f32) * steep).astype(bf16)
        delta_ref[here, :] = delta
        neigh_ref[here, :] = (delta.astype(f32) / degree_ref[here, 0:1]).astype(bf16)

    grad = contract_last(neigh_ref[...], w_neigh_ref[...]).astype(bf16)
    rest = width - FIRST
    for j in range(SPLIT):
        routed = contract_first(routing(j), grad).astype(bf16)
        first_ref[:, j * FIRST : (j + 1) * FIRST] = routed[:, :FIRST]
        second_ref[:, j * rest : (j + 1) * rest] = routed[:, FIRST:]


def middle(arrived, seeds, base, w_neigh, cotangent):
    sent = arrived.shape[0]
    seed_count, hidden = base.shape
    width = w_neigh.shape[0]
    return pl.pallas_call(
        middle_kernel,
        out_shape=[
            jax.ShapeDtypeStruct((seed_count, hidden), bf16),
            jax.ShapeDtypeStruct((seed_count, hidden), bf16),
            jax.ShapeDtypeStruct((seed_count, width), bf16),
            jax.ShapeDtypeStruct((sent, SPLIT * FIRST), bf16),
            jax.ShapeDtypeStruct((sent, SPLIT * (width - FIRST)), bf16),
        ],
        scratch_shapes=[
            pltpu.VMEM((seed_count, hidden), f32),
            pltpu.VMEM((seed_count, hidden), bf16),
            pltpu.VMEM((seed_count, EXTRA), f32),
        ],
        compiler_params=VMEM,
        cost_estimate=cost(
            4 * seed_count * width * (SPLIT * sent + hidden),
            2 * (2 * arrived.size + w_neigh.size + 5 * base.size),
        ),
    )(arrived, seeds, base, w_neigh, cotangent)


def terms_kernel(self_ref, aggregate_ref, delta_ref, out_ref):
    near, tall, hidden = out_ref.shape
    block = tall - MARGIN
    delta = delta_ref[...]
    half = near // 2
    for side, left in enumerate((self_ref, aggregate_ref)):
        product = contract_first(left[...], delta).astype(bf16)
        for b in range(half):
            out_ref[side * half + b, :block, :] = product[b * block : (b + 1) * block]
    column = jnp.sum(delta.astype(f32), axis=0, keepdims=True)
    first = lax.broadcasted_iota(jnp.int32, (MARGIN, hidden), 0) == 0
    margin = jnp.where(first, column, 0.0).astype(bf16)
    for b in range(near):
        out_ref[b, block:, :] = margin


def reduce_everywhere(self_rows, aggregate, delta):
    near = lax.axis_size(NEAR)
    far = lax.axis_size(FAR)
    seeds, width = self_rows.shape
    hidden = delta.shape[1]
    block = 2 * width // near
    piece = block // far
    terms = pl.pallas_call(
        terms_kernel,
        out_shape=jax.ShapeDtypeStruct((near, block + MARGIN, hidden), bf16),
        compiler_params=VMEM,
        cost_estimate=cost(4 * seeds * width * hidden, 8 * width * hidden),
    )(self_rows, aggregate, delta)
    summed = lax.psum_scatter(
        terms.reshape(-1, hidden), NEAR, scatter_dimension=0, tiled=True
    )
    pieces = jnp.concatenate(
        [
            summed[:block].reshape(far, piece, hidden),
            jnp.broadcast_to(summed[None, block : block + 2], (far, 2, hidden)),
        ],
        axis=1,
    )
    total = jnp.sum(exchange(pieces, FAR).astype(f32), axis=0)
    bias_total = total[piece]
    spread = exchange(
        jnp.broadcast_to(total.astype(bf16)[None], (far,) + total.shape), FAR
    )
    own = spread[:, :piece].reshape(block, hidden)
    full = lax.all_gather(own, NEAR, axis=0, tiled=True)
    return full, bias_total, spread


def after(value, earlier):
    def kernel(value_ref, earlier_ref, out_ref):
        pass

    return pl.pallas_call(
        kernel,
        in_specs=[pl.BlockSpec(memory_space=pl.ANY)] * 2,
        out_specs=pl.BlockSpec(memory_space=pl.ANY),
        out_shape=jax.ShapeDtypeStruct(value.shape, value.dtype),
        input_output_aliases={0: 0},
    )(value, earlier)


def on_device(
    feats, seed_rows, edge_rows, edge_slots, slot_seeds, w_self, w_neigh, bias, cotangent
):
    edge_rows = edge_rows[0]
    edge_slots = edge_slots[0]
    slot_seeds = slot_seeds[0]
    sources, slot_cap = slot_seeds.shape
    s_count = slot_cap // SPLIT
    seed_count = seed_rows.shape[0]
    row_count, width = feats.shape
    replicas = lax.axis_size("rep")
    select, partial_value = select_and_sum(feats, edge_rows, edge_slots, slot_cap)
    arrived = exchange(partial_value.reshape(sources, s_count, -1), DOM)
    seeds = slot_seeds.reshape(sources, SPLIT, s_count).transpose(1, 0, 2)
    seeds = seeds.reshape(SPLIT, 1, sources * s_count)
    self_rows = jnp.take(feats, seed_rows, axis=0)
    base = jnp.dot(self_rows, w_self, preferred_element_type=f32) + bias[None, :]
    hidden_out, delta, aggregate, first, second = middle(
        arrived.reshape(sources * s_count, -1), seeds, base, w_neigh, cotangent
    )

    def back(routed):
        columns = routed.shape[1] // SPLIT
        slot_grad = exchange(routed.reshape(sources, s_count, -1), DOM)
        slot_grad = slot_grad.reshape(sources * s_count, -1)
        local = sum(
            contract_first(select[j], slot_grad[:, j * columns : (j + 1) * columns])
            for j in range(SPLIT)
        )
        return local.astype(bf16)

    grads, bias_total, done = reduce_everywhere(self_rows, aggregate, delta)
    share1 = lax.psum_scatter(back(first), "rep", scatter_dimension=0, tiled=True)
    local2 = back(after(second, done))
    shares2 = exchange(local2.reshape(replicas, row_count // replicas, -1), "rep")
    share2 = jnp.sum(shares2.astype(f32), axis=0).astype(bf16)
    feat_grads = jnp.concatenate([share1, share2], axis=1)
    self_grad = contract_last(delta, w_self).astype(bf16)
    scale = float(seed_count * lax.axis_size(DOM) * replicas) ** (-0.5)
    grads = grads.astype(f32) * scale
    return (
        hidden_out,
        self_grad,
        feat_grads,
        grads[:width],
        grads[width:],
        bias_total * scale,
    )


def solution(mesh):
    fine = Mesh(
        np.asarray(mesh.devices).reshape(8, 4, 2, 4), ("z", "x", "c", "rep")
    )
    every = DOM + ("rep",)
    in_specs = (
        P(DOM, None),
        P(every),
        P(every, None, None),
        P(every, None, None),
        P(every, None, None),
        P(),
        P(),
        P(),
        P(every, None),
    )
    out_specs = (P(every, None), P(every, None), P(every, None), P(), P(), P())
    return jax.shard_map(
        on_device, mesh=fine, in_specs=in_specs, out_specs=out_specs, check_vma=False
    )
```

```python
import functools

import jax
import jax.numpy as jnp
import numpy as np
from jax import lax
from jax.experimental import pallas as pl
from jax.experimental.pallas import tpu as pltpu
from jax.sharding import Mesh, PartitionSpec as P

DOM = ("z", "x", "c")
NEAR = ("c", "rep")
bf16 = jnp.bfloat16
f32 = jnp.float32

GROUP = 4
STEP = 4
SPLIT = 4
EXTRA = 128
VMEM = pltpu.CompilerParams(vmem_limit_bytes=48 * 1024 * 1024)
MARGIN = 16


def contract_first(left, right):
    return lax.dot_general(
        left, right, (((0,), (0,)), ((), ())), preferred_element_type=f32
    )


def contract_last(left, right):
    return lax.dot_general(
        left, right, (((1,), (1,)), ((), ())), preferred_element_type=f32
    )


def exchange(value, axes):
    return lax.all_to_all(value, axes, split_axis=0, concat_axis=0, tiled=True)


def cost(flops, bytes_accessed):
    return pl.CostEstimate(flops=flops, bytes_accessed=bytes_accessed, transcendentals=0)


def select_kernel(rows_ref, keys_ref, feats_ref, select_ref, partial_ref):
    row_count, width = feats_ref.shape
    entries = rows_ref.shape[2]
    part = select_ref.shape[1] // STEP
    slots = SPLIT * part
    row_ids = lax.broadcasted_iota(jnp.int32, (row_count, entries), 0)
    slot_ids = lax.broadcasted_iota(jnp.int32, (slots, entries), 0)
    lanes = lax.broadcasted_iota(jnp.int32, (part, EXTRA), 1)
    for step in range(STEP):
        here = slice(step * part, (step + 1) * part)
        by_row = jnp.where(row_ids == rows_ref[step], 1.0, 0.0).astype(bf16)
        hits = jnp.where(slot_ids == keys_ref[step], 1.0, 0.0)
        chosen = contract_last(hits.astype(bf16), by_row).astype(bf16)
        count = jnp.sum(hits, axis=1, keepdims=True)
        tail = jnp.zeros((part, EXTRA), f32)
        for j in range(SPLIT):
            select_ref[j, here, :] = chosen[j * part : (j + 1) * part]
            tail = jnp.where(lanes == j, count[j * part : (j + 1) * part], tail)
        partial_ref[here, SPLIT * width :] = tail.astype(bf16)
    for j in range(SPLIT):
        partial_ref[:, j * width : (j + 1) * width] = jnp.dot(
            select_ref[j], feats_ref[...], preferred_element_type=f32
        ).astype(bf16)


def select_and_sum(feats, edge_rows, edge_slots, slot_cap):
    dests, entry_cap = edge_rows.shape
    row_count, width = feats.shape
    groups = dests // GROUP
    entries = GROUP * entry_cap
    s_count = slot_cap // SPLIT
    part = GROUP * s_count
    wide = SPLIT * width + EXTRA
    place = (jnp.arange(dests, dtype=jnp.int32) % GROUP * s_count)[:, None]
    keys = edge_slots // s_count * part + place + edge_slots % s_count
    keys = jnp.where(edge_slots < slot_cap, keys, -1)
    return pl.pallas_call(
        select_kernel,
        grid=(groups // STEP,),
        in_specs=[
            pl.BlockSpec((STEP, 1, entries), lambda i: (i, 0, 0)),
            pl.BlockSpec((STEP, 1, entries), lambda i: (i, 0, 0)),
            pl.BlockSpec((row_count, width), lambda i: (0, 0)),
        ],
        out_specs=[
            pl.BlockSpec((SPLIT, STEP * part, row_count), lambda i: (0, i, 0)),
            pl.BlockSpec((STEP * part, wide), lambda i: (i, 0)),
        ],
        out_shape=[
            jax.ShapeDtypeStruct((SPLIT, groups * part, row_count), bf16),
            jax.ShapeDtypeStruct((groups * part, wide), bf16),
        ],
        compiler_params=VMEM,
        cost_estimate=cost(
            2 * SPLIT * groups * part * row_count * (width + entries),
            2 * (row_count * width + groups * part * (SPLIT * row_count + wide)),
        ),
    )(
        edge_rows.reshape(groups, 1, entries),
        keys.reshape(groups, 1, entries),
        feats,
    )


def middle_kernel(
    arrived_ref,
    seeds_ref,
    base_ref,
    w_neigh_ref,
    cotangent_ref,
    hidden_ref,
    delta_ref,
    aggregate_ref,
    routed_ref,
    pre_ref,
    neigh_ref,
    degree_ref,
):
    seed_count = base_ref.shape[0]
    width = w_neigh_ref.shape[0]
    sent = seeds_ref.shape[2]
    ids = lax.broadcasted_iota(jnp.int32, (seed_count, sent), 0)
    lanes = lax.broadcasted_iota(jnp.int32, (seed_count, EXTRA), 1)

    def routing(j):
        return jnp.where(ids == seeds_ref[j], 1.0, 0.0).astype(bf16)

    total = jnp.zeros((seed_count, width), f32)
    counts = jnp.zeros((seed_count, EXTRA), f32)
    for j in range(SPLIT):
        route = routing(j)
        total += jnp.dot(
            route, arrived_ref[:, j * width : (j + 1) * width], preferred_element_type=f32
        )
        found = jnp.dot(route, arrived_ref[:, SPLIT * width :], preferred_element_type=f32)
        counts += jnp.where(lanes == j, found, 0.0)
    degree = jnp.maximum(jnp.sum(counts, axis=1, keepdims=True), 1.0)
    degree_ref[...] = jnp.broadcast_to(degree, (seed_count, EXTRA))
    aggregate_ref[...] = (total / degree).astype(bf16)
    pre_ref[...] = base_ref[...] + jnp.dot(
        aggregate_ref[...], w_neigh_ref[...], preferred_element_type=f32
    )

    rows = 16
    slope = (2.0 / np.pi) ** 0.5

    @pl.loop(0, seed_count // rows)
    def _(i):
        here = pl.ds(pl.multiple_of(i * rows, rows), rows)
        pre = pre_ref[here, :]
        square = pre * pre
        bend = jnp.tanh(slope * pre * (1.0 + 0.044715 * square))
        half = 0.5 * (1.0 + bend)
        hidden_ref[here, :] = (pre * half).astype(bf16)
        steep = half + 0.5 * pre * (1.0 - bend * bend) * (
            slope * (1.0 + 3 * 0.044715 * square)
        )
        delta = (cotangent_ref[here, :].astype(f32) * steep).astype(bf16)
        delta_ref[here, :] = delta
        neigh_ref[here, :] = (delta.astype(f32) / degree_ref[here, 0:1]).astype(bf16)

    grad = contract_last(neigh_ref[...], w_neigh_ref[...]).astype(bf16)
    for j in range(SPLIT):
        routed_ref[:, j * width : (j + 1) * width] = contract_first(
            routing(j), grad
        ).astype(bf16)


def middle(arrived, seeds, base, w_neigh, cotangent):
    sent = arrived.shape[0]
    seed_count, hidden = base.shape
    width = w_neigh.shape[0]
    return pl.pallas_call(
        middle_kernel,
        out_shape=[
            jax.ShapeDtypeStruct((seed_count, hidden), bf16),
            jax.ShapeDtypeStruct((seed_count, hidden), bf16),
            jax.ShapeDtypeStruct((seed_count, width), bf16),
            jax.ShapeDtypeStruct((sent, SPLIT * width), bf16),
        ],
        scratch_shapes=[
            pltpu.VMEM((seed_count, hidden), f32),
            pltpu.VMEM((seed_count, hidden), bf16),
            pltpu.VMEM((seed_count, EXTRA), f32),
        ],
        compiler_params=VMEM,
        cost_estimate=cost(
            4 * seed_count * width * (SPLIT * sent + hidden),
            2 * (2 * arrived.size + w_neigh.size + 5 * base.size),
        ),
    )(arrived, seeds, base, w_neigh, cotangent)


def terms_kernel(self_ref, aggregate_ref, delta_ref, out_ref):
    near, tall, hidden = out_ref.shape
    block = tall - MARGIN
    delta = delta_ref[...]
    half = near // 2
    for side, left in enumerate((self_ref, aggregate_ref)):
        product = contract_first(left[...], delta).astype(bf16)
        for b in range(half):
            out_ref[side * half + b, :block, :] = product[b * block : (b + 1) * block]
    column = jnp.sum(delta.astype(f32), axis=0, keepdims=True)
    first = lax.broadcasted_iota(jnp.int32, (MARGIN, hidden), 0) == 0
    margin = jnp.where(first, column, 0.0).astype(bf16)
    for b in range(near):
        out_ref[b, block:, :] = margin


def after(value, earlier):
    def kernel(value_ref, earlier_ref, out_ref):
        pass

    return pl.pallas_call(
        kernel,
        in_specs=[pl.BlockSpec(memory_space=pl.ANY)] * 2,
        out_specs=pl.BlockSpec(memory_space=pl.ANY),
        out_shape=jax.ShapeDtypeStruct(value.shape, value.dtype),
        input_output_aliases={0: 0},
    )(value, earlier)


def reduce_everywhere(self_rows, aggregate, delta, earlier):
    near = lax.axis_size(NEAR)
    seeds, width = self_rows.shape
    hidden = delta.shape[1]
    block = 2 * width // near
    terms = pl.pallas_call(
        terms_kernel,
        out_shape=jax.ShapeDtypeStruct((near, block + MARGIN, hidden), bf16),
        compiler_params=VMEM,
        cost_estimate=cost(4 * seeds * width * hidden, 8 * width * hidden),
    )(self_rows, aggregate, delta)
    summed = lax.psum_scatter(
        terms.reshape(-1, hidden), NEAR, scatter_dimension=0, tiled=True
    )
    part = block // lax.axis_size("x")
    parts = jnp.concatenate(
        [
            summed[:block].reshape(-1, part, hidden),
            jnp.broadcast_to(summed[None, block : block + 8], (block // part, 8, hidden)),
        ],
        axis=1,
    )
    line = lax.psum_scatter(
        parts.reshape(-1, hidden), "x", scatter_dimension=0, tiled=True
    )
    lines = lax.all_gather(after(line, earlier), "z", axis=0)
    total = jnp.sum(lines.astype(f32), axis=0)
    own = lax.all_gather(total[:part].astype(bf16), "x", axis=0, tiled=True)
    full = lax.all_gather(own, NEAR, axis=0, tiled=True)
    return full, total[part]


def scaled_kernel(scale, upper_ref, lower_ref, self_ref, neigh_ref):
    self_ref[...] = upper_ref[...].astype(f32) * scale
    neigh_ref[...] = lower_ref[...].astype(f32) * scale


def scaled_halves(full, scale):
    rows, hidden = full.shape
    half = rows // 2
    steps = 6
    tall = half // steps
    spec = pl.BlockSpec((tall, hidden), lambda i: (i, 0))
    return pl.pallas_call(
        functools.partial(scaled_kernel, scale),
        grid=(steps,),
        in_specs=[spec, pl.BlockSpec((tall, hidden), lambda i: (i + steps, 0))],
        out_specs=[spec, spec],
        out_shape=[jax.ShapeDtypeStruct((half, hidden), f32)] * 2,
        compiler_params=VMEM,
        cost_estimate=cost(rows * hidden, 6 * rows * hidden),
    )(full, full)


def scatter_kernel(select_ref, grad_ref, out_ref):
    width = out_ref.shape[1]
    total = contract_first(select_ref[0], grad_ref[:, :width])
    for j in range(1, SPLIT):
        total += contract_first(select_ref[j], grad_ref[:, j * width : (j + 1) * width])
    out_ref[...] = total.astype(bf16)


def scatter_sum(select, slot_grad):
    _, sent, rows = select.shape
    width = slot_grad.shape[1] // SPLIT
    return pl.pallas_call(
        scatter_kernel,
        out_shape=jax.ShapeDtypeStruct((rows, width), bf16),
        compiler_params=VMEM,
        cost_estimate=cost(
            2 * SPLIT * sent * rows * width, 2 * (select.size + slot_grad.size)
        ),
    )(select, slot_grad)


def on_device(
    feats, seed_rows, edge_rows, edge_slots, slot_seeds, w_self, w_neigh, bias, cotangent
):
    edge_rows = edge_rows[0]
    edge_slots = edge_slots[0]
    slot_seeds = slot_seeds[0]
    sources, slot_cap = slot_seeds.shape
    s_count = slot_cap // SPLIT
    seed_count = seed_rows.shape[0]
    row_count, width = feats.shape
    replicas = lax.axis_size("rep")
    select, partial_value = select_and_sum(feats, edge_rows, edge_slots, slot_cap)
    arrived = exchange(partial_value.reshape(sources, s_count, -1), DOM)
    seeds = slot_seeds.reshape(sources, SPLIT, s_count).transpose(1, 0, 2)
    seeds = seeds.reshape(SPLIT, 1, sources * s_count)
    self_rows = jnp.take(feats, seed_rows, axis=0)
    base = jnp.dot(self_rows, w_self, preferred_element_type=f32) + bias[None, :]
    hidden_out, delta, aggregate, routed = middle(
        arrived.reshape(sources * s_count, -1), seeds, base, w_neigh, cotangent
    )

    slot_grad = exchange(routed.reshape(sources, s_count, -1), DOM)
    full, bias_total = reduce_everywhere(self_rows, aggregate, delta, slot_grad)
    self_grad = contract_last(delta, w_self).astype(bf16)
    local = scatter_sum(select, slot_grad.reshape(sources * s_count, -1))
    shares = exchange(local.reshape(replicas, row_count // replicas, width), "rep")
    feat_grads = jnp.sum(shares.astype(f32), axis=0).astype(bf16)
    scale = float(seed_count * lax.axis_size(DOM) * replicas) ** (-0.5)
    grad_self, grad_neigh = scaled_halves(full, scale)
    return (
        hidden_out,
        self_grad,
        feat_grads,
        grad_self,
        grad_neigh,
        bias_total * scale,
    )


def solution(mesh):
    fine = Mesh(
        np.asarray(mesh.devices).reshape(8, 4, 2, 4), ("z", "x", "c", "rep")
    )
    every = DOM + ("rep",)
    in_specs = (
        P(DOM, None),
        P(every),
        P(every, None, None),
        P(every, None, None),
        P(every, None, None),
        P(),
        P(),
        P(),
        P(every, None),
    )
    out_specs = (P(every, None), P(every, None), P(every, None), P(), P(), P())
    return jax.shard_map(
        on_device, mesh=fine, in_specs=in_specs, out_specs=out_specs, check_vma=False
    )
```

```python
import functools

import jax
import jax.numpy as jnp
import numpy as np
from jax import lax
from jax.experimental import pallas as pl
from jax.experimental.pallas import tpu as pltpu
from jax.sharding import Mesh, PartitionSpec as P

DOM = ("z", "x", "c")
NEAR = ("c", "rep")
bf16 = jnp.bfloat16
f32 = jnp.float32

GROUP = 4
STEP = 4
SPLIT = 4
EXTRA = 128
VMEM = pltpu.CompilerParams(vmem_limit_bytes=60 * 1024 * 1024)
MARGIN = 16


def contract_first(left, right):
    return lax.dot_general(
        left, right, (((0,), (0,)), ((), ())), preferred_element_type=f32
    )


def contract_last(left, right):
    return lax.dot_general(
        left, right, (((1,), (1,)), ((), ())), preferred_element_type=f32
    )


def exchange(value, axes):
    return lax.all_to_all(value, axes, split_axis=0, concat_axis=0, tiled=True)


def spread(value, axes):
    return jnp.broadcast_to(value[None], (lax.axis_size(axes),) + value.shape)


def cost(flops, bytes_accessed):
    return pl.CostEstimate(flops=flops, bytes_accessed=bytes_accessed, transcendentals=0)


def select_kernel(rows_ref, keys_ref, feats_ref, select_ref, partial_ref):
    row_count, width = feats_ref.shape
    entries = rows_ref.shape[2]
    part = select_ref.shape[1] // STEP
    slots = SPLIT * part
    row_ids = lax.broadcasted_iota(jnp.int32, (row_count, entries), 0)
    slot_ids = lax.broadcasted_iota(jnp.int32, (slots, entries), 0)
    lanes = lax.broadcasted_iota(jnp.int32, (part, EXTRA), 1)
    for step in range(STEP):
        here = slice(step * part, (step + 1) * part)
        by_row = jnp.where(row_ids == rows_ref[step], 1.0, 0.0).astype(bf16)
        hits = jnp.where(slot_ids == keys_ref[step], 1.0, 0.0)
        chosen = contract_last(hits.astype(bf16), by_row).astype(bf16)
        count = jnp.sum(hits, axis=1, keepdims=True)
        tail = jnp.zeros((part, EXTRA), f32)
        for j in range(SPLIT):
            select_ref[j, here, :] = chosen[j * part : (j + 1) * part]
            tail = jnp.where(lanes == j, count[j * part : (j + 1) * part], tail)
        partial_ref[here, SPLIT * width :] = tail.astype(bf16)
    for j in range(SPLIT):
        partial_ref[:, j * width : (j + 1) * width] = jnp.dot(
            select_ref[j], feats_ref[...], preferred_element_type=f32
        ).astype(bf16)


def select_and_sum(feats, edge_rows, edge_slots, slot_cap):
    dests, entry_cap = edge_rows.shape
    row_count, width = feats.shape
    groups = dests // GROUP
    entries = GROUP * entry_cap
    s_count = slot_cap // SPLIT
    part = GROUP * s_count
    wide = SPLIT * width + EXTRA
    place = (jnp.arange(dests, dtype=jnp.int32) % GROUP * s_count)[:, None]
    keys = edge_slots // s_count * part + place + edge_slots % s_count
    keys = jnp.where(edge_slots < slot_cap, keys, -1)
    return pl.pallas_call(
        select_kernel,
        grid=(groups // STEP,),
        in_specs=[
            pl.BlockSpec((STEP, 1, entries), lambda i: (i, 0, 0)),
            pl.BlockSpec((STEP, 1, entries), lambda i: (i, 0, 0)),
            pl.BlockSpec((row_count, width), lambda i: (0, 0)),
        ],
        out_specs=[
            pl.BlockSpec((SPLIT, STEP * part, row_count), lambda i: (0, i, 0)),
            pl.BlockSpec((STEP * part, wide), lambda i: (i, 0)),
        ],
        out_shape=[
            jax.ShapeDtypeStruct((SPLIT, groups * part, row_count), bf16),
            jax.ShapeDtypeStruct((groups * part, wide), bf16),
        ],
        compiler_params=VMEM,
        cost_estimate=cost(
            2 * SPLIT * groups * part * row_count * (width + entries),
            2 * (row_count * width + groups * part * (SPLIT * row_count + wide)),
        ),
    )(
        edge_rows.reshape(groups, 1, entries),
        keys.reshape(groups, 1, entries),
        feats,
    )


def middle_kernel(
    arrived_ref,
    seeds_ref,
    base_ref,
    w_neigh_ref,
    cotangent_ref,
    hidden_ref,
    delta_ref,
    aggregate_ref,
    routed_ref,
    pre_ref,
    neigh_ref,
    degree_ref,
):
    seed_count = base_ref.shape[0]
    width = w_neigh_ref.shape[0]
    sent = seeds_ref.shape[2]
    ids = lax.broadcasted_iota(jnp.int32, (seed_count, sent), 0)
    lanes = lax.broadcasted_iota(jnp.int32, (seed_count, EXTRA), 1)

    def routing(j):
        return jnp.where(ids == seeds_ref[j], 1.0, 0.0).astype(bf16)

    total = jnp.zeros((seed_count, width), f32)
    counts = jnp.zeros((seed_count, EXTRA), f32)
    for j in range(SPLIT):
        route = routing(j)
        total += jnp.dot(
            route, arrived_ref[:, j * width : (j + 1) * width], preferred_element_type=f32
        )
        found = jnp.dot(route, arrived_ref[:, SPLIT * width :], preferred_element_type=f32)
        counts += jnp.where(lanes == j, found, 0.0)
    degree = jnp.maximum(jnp.sum(counts, axis=1, keepdims=True), 1.0)
    degree_ref[...] = jnp.broadcast_to(degree, (seed_count, EXTRA))
    aggregate_ref[...] = (total / degree).astype(bf16)
    pre_ref[...] = base_ref[...] + jnp.dot(
        aggregate_ref[...], w_neigh_ref[...], preferred_element_type=f32
    )

    rows = 16
    slope = (2.0 / np.pi) ** 0.5

    @pl.loop(0, seed_count // rows)
    def _(i):
        here = pl.ds(pl.multiple_of(i * rows, rows), rows)
        pre = pre_ref[here, :]
        square = pre * pre
        bend = jnp.tanh(slope * pre * (1.0 + 0.044715 * square))
        half = 0.5 * (1.0 + bend)
        hidden_ref[here, :] = (pre * half).astype(bf16)
        steep = half + 0.5 * pre * (1.0 - bend * bend) * (
            slope * (1.0 + 3 * 0.044715 * square)
        )
        delta = (cotangent_ref[here, :].astype(f32) * steep).astype(bf16)
        delta_ref[here, :] = delta
        neigh_ref[here, :] = (delta.astype(f32) / degree_ref[here, 0:1]).astype(bf16)

    grad = contract_last(neigh_ref[...], w_neigh_ref[...]).astype(bf16)
    for j in range(SPLIT):
        routed_ref[:, j * width : (j + 1) * width] = contract_first(
            routing(j), grad
        ).astype(bf16)


def middle(arrived, seeds, base, w_neigh, cotangent):
    sent = arrived.shape[0]
    seed_count, hidden = base.shape
    width = w_neigh.shape[0]
    return pl.pallas_call(
        middle_kernel,
        out_shape=[
            jax.ShapeDtypeStruct((seed_count, hidden), bf16),
            jax.ShapeDtypeStruct((seed_count, hidden), bf16),
            jax.ShapeDtypeStruct((seed_count, width), bf16),
            jax.ShapeDtypeStruct((sent, SPLIT * width), bf16),
        ],
        scratch_shapes=[
            pltpu.VMEM((seed_count, hidden), f32),
            pltpu.VMEM((seed_count, hidden), bf16),
            pltpu.VMEM((seed_count, EXTRA), f32),
        ],
        compiler_params=VMEM,
        cost_estimate=cost(
            4 * seed_count * width * (SPLIT * sent + hidden),
            2 * (2 * arrived.size + w_neigh.size + 5 * base.size),
        ),
    )(arrived, seeds, base, w_neigh, cotangent)


def terms_kernel(self_ref, aggregate_ref, delta_ref, out_ref):
    near, tall, hidden = out_ref.shape
    block = tall - MARGIN
    delta = delta_ref[...]
    half = near // 2
    for side, left in enumerate((self_ref, aggregate_ref)):
        product = contract_first(left[...], delta).astype(bf16)
        for b in range(half):
            out_ref[side * half + b, :block, :] = product[b * block : (b + 1) * block]
    column = jnp.sum(delta.astype(f32), axis=0, keepdims=True)
    first = lax.broadcasted_iota(jnp.int32, (MARGIN, hidden), 0) == 0
    margin = jnp.where(first, column, 0.0).astype(bf16)
    for b in range(near):
        out_ref[b, block:, :] = margin


def after(value, earlier):
    def kernel(value_ref, earlier_ref, out_ref):
        pass

    return pl.pallas_call(
        kernel,
        in_specs=[pl.BlockSpec(memory_space=pl.ANY)] * 2,
        out_specs=pl.BlockSpec(memory_space=pl.ANY),
        out_shape=jax.ShapeDtypeStruct(value.shape, value.dtype),
        input_output_aliases={0: 0},
    )(value, earlier)


def reduce_everywhere(self_rows, aggregate, delta, earlier):
    near = lax.axis_size(NEAR)
    seeds, width = self_rows.shape
    hidden = delta.shape[1]
    block = 2 * width // near
    terms = pl.pallas_call(
        terms_kernel,
        out_shape=jax.ShapeDtypeStruct((near, block + MARGIN, hidden), bf16),
        compiler_params=VMEM,
        cost_estimate=cost(4 * seeds * width * hidden, 8 * width * hidden),
    )(self_rows, aggregate, delta)
    summed = lax.psum_scatter(
        terms.reshape(-1, hidden), NEAR, scatter_dimension=0, tiled=True
    )
    height = lax.axis_size("z")
    part = block // height
    parts = jnp.concatenate(
        [
            summed[:block].reshape(height, part, hidden),
            jnp.broadcast_to(summed[None, block : block + 8], (height, 8, hidden)),
        ],
        axis=1,
    )
    line = lax.psum_scatter(
        parts.reshape(-1, hidden), "z", scatter_dimension=0, tiled=True
    )
    lines = exchange(spread(after(line, earlier), "x"), "x")
    total = jnp.sum(lines.astype(f32), axis=0)
    own = exchange(spread(total.astype(bf16), "z"), "z")
    margin = jnp.concatenate([own[0, part:]] * (MARGIN // 8), axis=0)
    own = jnp.concatenate([own[:, :part].reshape(block, hidden), margin], axis=0)
    return lax.all_gather(own, NEAR, axis=0, tiled=True)


def scaled_kernel(scale, upper_ref, lower_ref, self_ref, neigh_ref, bias_ref):
    block = self_ref.shape[0]
    self_ref[...] = upper_ref[:block, :].astype(f32) * scale
    neigh_ref[...] = lower_ref[:block, :].astype(f32) * scale

    @pl.when(pl.program_id(0) == 0)
    def _():
        bias_ref[...] = upper_ref[block:, :].astype(f32) * scale


def scaled_parts(full, width, scale):
    hidden = full.shape[1]
    near = lax.axis_size(NEAR)
    tall = full.shape[0] // near
    half = near // 2
    block = width // half
    grad_spec = pl.BlockSpec((block, hidden), lambda i: (i, 0))
    return pl.pallas_call(
        functools.partial(scaled_kernel, scale),
        grid=(half,),
        in_specs=[
            pl.BlockSpec((tall, hidden), lambda i: (i, 0)),
            pl.BlockSpec((tall, hidden), lambda i: (i + half, 0)),
        ],
        out_specs=[
            grad_spec,
            grad_spec,
            pl.BlockSpec((MARGIN, hidden), lambda i: (0, 0)),
        ],
        out_shape=[
            jax.ShapeDtypeStruct((width, hidden), f32),
            jax.ShapeDtypeStruct((width, hidden), f32),
            jax.ShapeDtypeStruct((MARGIN, hidden), f32),
        ],
        compiler_params=VMEM,
        cost_estimate=cost(full.size, 6 * full.size),
    )(full, full)


def scatter_kernel(select_ref, grad_ref, out_ref):
    width = out_ref.shape[1]
    total = contract_first(select_ref[0], grad_ref[:, :width])
    for j in range(1, SPLIT):
        total += contract_first(select_ref[j], grad_ref[:, j * width : (j + 1) * width])
    out_ref[...] = total.astype(bf16)


def scatter_sum(select, slot_grad):
    _, sent, rows = select.shape
    width = slot_grad.shape[1] // SPLIT
    return pl.pallas_call(
        scatter_kernel,
        out_shape=jax.ShapeDtypeStruct((rows, width), bf16),
        compiler_params=VMEM,
        cost_estimate=cost(
            2 * SPLIT * sent * rows * width, 2 * (select.size + slot_grad.size)
        ),
    )(select, slot_grad)


def on_device(
    feats, seed_rows, edge_rows, edge_slots, slot_seeds, w_self, w_neigh, bias, cotangent
):
    edge_rows = edge_rows[0]
    edge_slots = edge_slots[0]
    slot_seeds = slot_seeds[0]
    sources, slot_cap = slot_seeds.shape
    s_count = slot_cap // SPLIT
    seed_count = seed_rows.shape[0]
    row_count, width = feats.shape
    replicas = lax.axis_size("rep")
    select, partial_value = select_and_sum(feats, edge_rows, edge_slots, slot_cap)
    arrived = exchange(partial_value.reshape(sources, s_count, -1), DOM)
    seeds = slot_seeds.reshape(sources, SPLIT, s_count).transpose(1, 0, 2)
    seeds = seeds.reshape(SPLIT, 1, sources * s_count)
    self_rows = jnp.take(feats, seed_rows, axis=0)
    base = jnp.dot(self_rows, w_self, preferred_element_type=f32) + bias[None, :]
    hidden_out, delta, aggregate, routed = middle(
        arrived.reshape(sources * s_count, -1), seeds, base, w_neigh, cotangent
    )

    slot_grad = exchange(routed.reshape(sources, s_count, -1), DOM)
    full = reduce_everywhere(self_rows, aggregate, delta, slot_grad)
    self_grad = contract_last(delta, w_self).astype(bf16)
    local = scatter_sum(select, slot_grad.reshape(sources * s_count, -1))
    shares = exchange(local.reshape(replicas, row_count // replicas, width), "rep")
    feat_grads = jnp.sum(shares.astype(f32), axis=0).astype(bf16)
    scale = float(seed_count * lax.axis_size(DOM) * replicas) ** (-0.5)
    grad_self, grad_neigh, grad_bias = scaled_parts(full, width, scale)
    return (
        hidden_out,
        self_grad,
        feat_grads,
        grad_self,
        grad_neigh,
        grad_bias[0],
    )


def solution(mesh):
    fine = Mesh(
        np.asarray(mesh.devices).reshape(8, 4, 2, 4), ("z", "x", "c", "rep")
    )
    every = DOM + ("rep",)
    in_specs = (
        P(DOM, None),
        P(every),
        P(every, None, None),
        P(every, None, None),
        P(every, None, None),
        P(),
        P(),
        P(),
        P(every, None),
    )
    out_specs = (P(every, None), P(every, None), P(every, None), P(), P(), P())
    return jax.shard_map(
        on_device, mesh=fine, in_specs=in_specs, out_specs=out_specs, check_vma=False
    )
```

```python
import functools

import jax
import jax.numpy as jnp
import numpy as np
from jax import lax
from jax.experimental import pallas as pl
from jax.experimental.pallas import tpu as pltpu
from jax.sharding import Mesh, PartitionSpec as P

DOM = ("z", "x", "c")
NEAR = ("c", "rep")
FAR = ("x", "z")
bf16 = jnp.bfloat16
f32 = jnp.float32

GROUP = 4
STEP = 4
SPLIT = 4
EXTRA = 128
VMEM = pltpu.CompilerParams(vmem_limit_bytes=60 * 1024 * 1024)
MARGIN = 16


def contract_first(left, right):
    return lax.dot_general(
        left, right, (((0,), (0,)), ((), ())), preferred_element_type=f32
    )


def contract_last(left, right):
    return lax.dot_general(
        left, right, (((1,), (1,)), ((), ())), preferred_element_type=f32
    )


def exchange(value, axes):
    return lax.all_to_all(value, axes, split_axis=0, concat_axis=0, tiled=True)


def spread(value, axes):
    return jnp.broadcast_to(value[None], (lax.axis_size(axes),) + value.shape)


def cost(flops, bytes_accessed):
    return pl.CostEstimate(flops=flops, bytes_accessed=bytes_accessed, transcendentals=0)


def select_kernel(rows_ref, slots_ref, feats_ref, select_ref, partial_ref):
    row_count, width = feats_ref.shape
    dests, entry_cap = rows_ref.shape
    entries = GROUP * entry_cap
    part = select_ref.shape[1] // STEP
    s_count = part // GROUP
    slots = SPLIT * part
    named = slots_ref[...]
    place = lax.broadcasted_iota(jnp.int32, named.shape, 0) % GROUP * s_count
    keys = named // s_count * part + place + named % s_count
    keys = jnp.where(named < SPLIT * s_count, keys, -1)
    row_ids = lax.broadcasted_iota(jnp.int32, (row_count, entries), 0)
    slot_ids = lax.broadcasted_iota(jnp.int32, (slots, entries), 0)
    lanes = lax.broadcasted_iota(jnp.int32, (part, EXTRA), 1)

    def side_by_side(values, step):
        first = step * GROUP
        return jnp.concatenate(
            [values[first + i : first + i + 1] for i in range(GROUP)], axis=1
        )

    for step in range(STEP):
        here = slice(step * part, (step + 1) * part)
        by_row = jnp.where(row_ids == side_by_side(rows_ref[...], step), 1.0, 0.0)
        hits = jnp.where(slot_ids == side_by_side(keys, step), 1.0, 0.0)
        chosen = contract_last(hits.astype(bf16), by_row.astype(bf16)).astype(bf16)
        count = jnp.sum(hits, axis=1, keepdims=True)
        tail = jnp.zeros((part, EXTRA), f32)
        for j in range(SPLIT):
            select_ref[j, here, :] = chosen[j * part : (j + 1) * part]
            tail = jnp.where(lanes == j, count[j * part : (j + 1) * part], tail)
        partial_ref[here, SPLIT * width :] = tail.astype(bf16)
    for j in range(SPLIT):
        partial_ref[:, j * width : (j + 1) * width] = jnp.dot(
            select_ref[j], feats_ref[...], preferred_element_type=f32
        ).astype(bf16)


def select_and_sum(feats, edge_rows, edge_slots, slot_cap):
    dests, entry_cap = edge_rows.shape
    row_count, width = feats.shape
    s_count = slot_cap // SPLIT
    sent = dests * s_count
    steps = dests // (GROUP * STEP)
    wide = SPLIT * width + EXTRA
    edge_spec = pl.BlockSpec((GROUP * STEP, entry_cap), lambda i: (i, 0))
    return pl.pallas_call(
        select_kernel,
        grid=(steps,),
        in_specs=[
            edge_spec,
            edge_spec,
            pl.BlockSpec((row_count, width), lambda i: (0, 0)),
        ],
        out_specs=[
            pl.BlockSpec((SPLIT, sent // steps, row_count), lambda i: (0, i, 0)),
            pl.BlockSpec((sent // steps, wide), lambda i: (i, 0)),
        ],
        out_shape=[
            jax.ShapeDtypeStruct((SPLIT, sent, row_count), bf16),
            jax.ShapeDtypeStruct((sent, wide), bf16),
        ],
        compiler_params=VMEM,
        cost_estimate=cost(
            2 * SPLIT * sent * row_count * (width + GROUP * entry_cap),
            2 * (row_count * width + sent * (SPLIT * row_count + wide)),
        ),
    )(edge_rows, edge_slots, feats)


def middle_kernel(
    arrived_any,
    seeds_ref,
    base_ref,
    w_neigh_ref,
    cotangent_ref,
    self_ref,
    hidden_ref,
    delta_ref,
    routed_any,
    terms_any,
    arrived_ref,
    routed_ref,
    terms_ref,
    aggregate_ref,
    pre_ref,
    neigh_ref,
    degree_ref,
    in_sems,
    out_sems,
):
    seed_count = base_ref.shape[0]
    width = w_neigh_ref.shape[0]
    sent = seeds_ref.shape[2]
    near, tall, hidden = terms_ref.shape
    block = tall - MARGIN
    ids = lax.broadcasted_iota(jnp.int32, (seed_count, sent), 0)
    lanes = lax.broadcasted_iota(jnp.int32, (seed_count, EXTRA), 1)

    def columns(j):
        return slice(j * width, (j + 1) * width if j < SPLIT else j * width + EXTRA)

    def routing(j):
        return jnp.where(ids == seeds_ref[j], 1.0, 0.0).astype(bf16)

    loads = [
        pltpu.make_async_copy(
            arrived_any.at[:, columns(j)], arrived_ref.at[:, columns(j)], in_sems.at[j]
        )
        for j in range(SPLIT + 1)
    ]
    loads[SPLIT].start()
    for j in range(SPLIT):
        loads[j].start()

    total = jnp.zeros((seed_count, width), f32)
    counts = jnp.zeros((seed_count, EXTRA), f32)
    loads[SPLIT].wait()
    for j in range(SPLIT):
        route = routing(j)
        loads[j].wait()
        total += jnp.dot(route, arrived_ref[:, columns(j)], preferred_element_type=f32)
        found = jnp.dot(
            route, arrived_ref[:, columns(SPLIT)], preferred_element_type=f32
        )
        counts += jnp.where(lanes == j, found, 0.0)
    degree = jnp.maximum(jnp.sum(counts, axis=1, keepdims=True), 1.0)
    degree_ref[...] = jnp.broadcast_to(degree, (seed_count, EXTRA))
    aggregate_ref[...] = (total / degree).astype(bf16)
    pre_ref[...] = base_ref[...] + jnp.dot(
        aggregate_ref[...], w_neigh_ref[...], preferred_element_type=f32
    )

    rows = 16
    slope = (2.0 / np.pi) ** 0.5

    @pl.loop(0, seed_count // rows)
    def _(i):
        here = pl.ds(pl.multiple_of(i * rows, rows), rows)
        pre = pre_ref[here, :]
        square = pre * pre
        bend = jnp.tanh(slope * pre * (1.0 + 0.044715 * square))
        half = 0.5 * (1.0 + bend)
        hidden_ref[here, :] = (pre * half).astype(bf16)
        steep = half + 0.5 * pre * (1.0 - bend * bend) * (
            slope * (1.0 + 3 * 0.044715 * square)
        )
        delta = (cotangent_ref[here, :].astype(f32) * steep).astype(bf16)
        delta_ref[here, :] = delta
        neigh_ref[here, :] = (delta.astype(f32) / degree_ref[here, 0:1]).astype(bf16)

    copies = []

    def send(source, target):
        copy = pltpu.make_async_copy(source, target, out_sems.at[len(copies)])
        copy.start()
        copies.append(copy)

    grad = contract_last(neigh_ref[...], w_neigh_ref[...]).astype(bf16)
    for j in range(SPLIT):
        routed_ref[:, columns(j)] = contract_first(routing(j), grad).astype(bf16)
        send(routed_ref.at[:, columns(j)], routed_any.at[:, columns(j)])

    delta = delta_ref[...]
    column = jnp.sum(delta.astype(f32), axis=0, keepdims=True)
    first = lax.broadcasted_iota(jnp.int32, (MARGIN, hidden), 0) == 0
    margin = jnp.where(first, column, 0.0).astype(bf16)
    half = near // 2
    for side, left in enumerate((self_ref, aggregate_ref)):
        product = contract_first(left[...], delta).astype(bf16)
        mine = slice(side * half, (side + 1) * half)
        for b in range(half):
            terms_ref[side * half + b, :block, :] = product[b * block : (b + 1) * block]
            terms_ref[side * half + b, block:, :] = margin
        send(terms_ref.at[mine], terms_any.at[mine])
    for copy in copies:
        copy.wait()


def middle(arrived, seeds, base, w_neigh, cotangent, self_rows):
    sent, wide = arrived.shape
    seed_count, hidden = base.shape
    width = w_neigh.shape[0]
    near = lax.axis_size(NEAR)
    terms = (near, 2 * width // near + MARGIN, hidden)
    vmem = pl.BlockSpec(memory_space=pltpu.VMEM)
    hbm = pl.BlockSpec(memory_space=pltpu.HBM)
    return pl.pallas_call(
        middle_kernel,
        in_specs=[hbm] + [vmem] * 5,
        out_specs=[vmem, vmem, hbm, hbm],
        out_shape=[
            jax.ShapeDtypeStruct((seed_count, hidden), bf16),
            jax.ShapeDtypeStruct((seed_count, hidden), bf16),
            jax.ShapeDtypeStruct((sent, SPLIT * width), bf16),
            jax.ShapeDtypeStruct(terms, bf16),
        ],
        scratch_shapes=[
            pltpu.VMEM((sent, wide), bf16),
            pltpu.VMEM((sent, SPLIT * width), bf16),
            pltpu.VMEM(terms, bf16),
            pltpu.VMEM((seed_count, width), bf16),
            pltpu.VMEM((seed_count, hidden), f32),
            pltpu.VMEM((seed_count, hidden), bf16),
            pltpu.VMEM((seed_count, EXTRA), f32),
            pltpu.SemaphoreType.DMA((SPLIT + 1,)),
            pltpu.SemaphoreType.DMA((SPLIT + 2,)),
        ],
        compiler_params=pltpu.CompilerParams(vmem_limit_bytes=40 * 1024 * 1024),
        cost_estimate=cost(
            4 * seed_count * width * (SPLIT * sent + 2 * hidden),
            2 * (2 * arrived.size + 3 * w_neigh.size + 5 * base.size),
        ),
    )(arrived, seeds, base, w_neigh, cotangent, self_rows)


def after(value, earlier):
    def kernel(value_ref, earlier_ref, out_ref):
        pass

    return pl.pallas_call(
        kernel,
        in_specs=[pl.BlockSpec(memory_space=pl.ANY)] * 2,
        out_specs=pl.BlockSpec(memory_space=pl.ANY),
        out_shape=jax.ShapeDtypeStruct(value.shape, value.dtype),
        input_output_aliases={0: 0},
    )(value, earlier)


def reduce_everywhere(terms, earlier, meanwhile):
    _, tall, hidden = terms.shape
    block = tall - MARGIN
    part = block // lax.axis_size("x")
    piece = part // lax.axis_size("z")
    summed = lax.psum_scatter(
        terms.reshape(-1, hidden), NEAR, scatter_dimension=0, tiled=True
    )
    parts = summed[:block].reshape(-1, part, hidden)
    margin = summed[None, block : block + 8]
    parts = jnp.concatenate([parts, jnp.repeat(margin, block // part, axis=0)], axis=1)
    line = lax.psum_scatter(
        parts.reshape(-1, hidden), "x", scatter_dimension=0, tiled=True
    )
    line = after(line, earlier)
    pieces = line[:part].reshape(-1, piece, hidden)
    margin = line[None, part : part + 2]
    pieces = jnp.concatenate([pieces, jnp.repeat(margin, part // piece, axis=0)], axis=1)
    total = jnp.sum(exchange(pieces, "z").astype(f32), axis=0).astype(bf16)
    own = exchange(spread(total, FAR), FAR)
    margin = jnp.concatenate([own[0, piece:]] * (MARGIN // 2), axis=0)
    own = jnp.concatenate([own[:, :piece].reshape(block, hidden), margin], axis=0)
    return lax.all_gather(after(own, meanwhile), NEAR, axis=0, tiled=True)


def scaled_kernel(scale, upper_ref, lower_ref, self_ref, neigh_ref, bias_ref):
    block = self_ref.shape[0]
    self_ref[...] = upper_ref[:block, :].astype(f32) * scale
    neigh_ref[...] = lower_ref[:block, :].astype(f32) * scale

    @pl.when(pl.program_id(0) == 0)
    def _():
        bias_ref[...] = upper_ref[block : block + MARGIN, :].astype(f32)[0:1] * scale


def scaled_parts(full, width, scale):
    hidden = full.shape[1]
    near = lax.axis_size(NEAR)
    tall = full.shape[0] // near
    half = near // 2
    block = width // half
    grad_spec = pl.BlockSpec((block, hidden), lambda i: (i, 0))
    return pl.pallas_call(
        functools.partial(scaled_kernel, scale),
        grid=(half,),
        in_specs=[
            pl.BlockSpec((tall, hidden), lambda i: (i, 0)),
            pl.BlockSpec((tall, hidden), lambda i: (i + half, 0)),
        ],
        out_specs=[
            grad_spec,
            grad_spec,
            pl.BlockSpec((1, hidden), lambda i: (0, 0)),
        ],
        out_shape=[
            jax.ShapeDtypeStruct((width, hidden), f32),
            jax.ShapeDtypeStruct((width, hidden), f32),
            jax.ShapeDtypeStruct((1, hidden), f32),
        ],
        compiler_params=VMEM,
        cost_estimate=cost(full.size, 6 * full.size),
    )(full, full)


def scatter_kernel(select_ref, grad_ref, out_ref):
    width = out_ref.shape[1]
    total = contract_first(select_ref[0], grad_ref[:, :width])
    for j in range(1, SPLIT):
        total += contract_first(select_ref[j], grad_ref[:, j * width : (j + 1) * width])
    out_ref[...] = total.astype(bf16)


def scatter_sum(select, slot_grad):
    _, sent, rows = select.shape
    width = slot_grad.shape[1] // SPLIT
    return pl.pallas_call(
        scatter_kernel,
        out_shape=jax.ShapeDtypeStruct((rows, width), bf16),
        compiler_params=VMEM,
        cost_estimate=cost(
            2 * SPLIT * sent * rows * width, 2 * (select.size + slot_grad.size)
        ),
    )(select, slot_grad)


def on_device(
    feats, seed_rows, edge_rows, edge_slots, slot_seeds, w_self, w_neigh, bias, cotangent
):
    edge_rows = edge_rows[0]
    edge_slots = edge_slots[0]
    slot_seeds = slot_seeds[0]
    sources, slot_cap = slot_seeds.shape
    s_count = slot_cap // SPLIT
    seed_count = seed_rows.shape[0]
    width = feats.shape[1]
    replicas = lax.axis_size("rep")
    select, partial_value = select_and_sum(feats, edge_rows, edge_slots, slot_cap)
    arrived = exchange(partial_value.reshape(sources, s_count, -1), DOM)
    seeds = slot_seeds.reshape(sources, SPLIT, s_count).transpose(1, 0, 2)
    seeds = seeds.reshape(SPLIT, 1, sources * s_count)
    self_rows = jnp.take(feats, seed_rows, axis=0)
    base = jnp.dot(self_rows, w_self, preferred_element_type=f32) + bias[None, :]
    hidden_out, delta, routed, terms = middle(
        arrived.reshape(sources * s_count, -1), seeds, base, w_neigh, cotangent, self_rows
    )

    slot_grad = exchange(routed.reshape(sources, s_count, -1), DOM)
    self_grad = contract_last(delta, w_self).astype(bf16)
    local = scatter_sum(select, slot_grad.reshape(sources * s_count, -1))
    feat_grads = lax.psum_scatter(local, "rep", scatter_dimension=0, tiled=True)
    full = reduce_everywhere(terms, slot_grad, feat_grads)
    scale = float(seed_count * lax.axis_size(DOM) * replicas) ** (-0.5)
    grad_self, grad_neigh, grad_bias = scaled_parts(full, width, scale)
    return (
        hidden_out,
        self_grad,
        feat_grads,
        grad_self,
        grad_neigh,
        grad_bias.reshape(-1),
    )


def solution(mesh):
    fine = Mesh(
        np.asarray(mesh.devices).reshape(8, 4, 2, 4), ("z", "x", "c", "rep")
    )
    every = DOM + ("rep",)
    in_specs = (
        P(DOM, None),
        P(every),
        P(every, None, None),
        P(every, None, None),
        P(every, None, None),
        P(),
        P(),
        P(),
        P(every, None),
    )
    out_specs = (P(every, None), P(every, None), P(every, None), P(), P(), P())
    return jax.shard_map(
        on_device, mesh=fine, in_specs=in_specs, out_specs=out_specs, check_vma=False
    )
```

```python
import functools

import jax
import jax.numpy as jnp
import numpy as np
from jax import lax
from jax.experimental import pallas as pl
from jax.experimental.pallas import tpu as pltpu
from jax.sharding import Mesh, PartitionSpec as P

DOM = ("z", "x", "c")
NEAR = ("c", "rep")
FAR = ("x", "z")
bf16 = jnp.bfloat16
f32 = jnp.float32

GROUP = 4
STEP = 4
SPLIT = 4
EXTRA = 128
VMEM = pltpu.CompilerParams(vmem_limit_bytes=60 * 1024 * 1024)
MARGIN = 16


def contract_first(left, right):
    return lax.dot_general(
        left, right, (((0,), (0,)), ((), ())), preferred_element_type=f32
    )


def contract_last(left, right):
    return lax.dot_general(
        left, right, (((1,), (1,)), ((), ())), preferred_element_type=f32
    )


def exchange(value, axes):
    return lax.all_to_all(value, axes, split_axis=0, concat_axis=0, tiled=True)


def spread(value, axes):
    return jnp.broadcast_to(value[None], (lax.axis_size(axes),) + value.shape)


def cost(flops, bytes_accessed):
    return pl.CostEstimate(flops=flops, bytes_accessed=bytes_accessed, transcendentals=0)


def select_kernel(rows_ref, slots_ref, feats_ref, select_ref, partial_ref):
    row_count, width = feats_ref.shape
    dests, entry_cap = rows_ref.shape
    entries = GROUP * entry_cap
    part = select_ref.shape[1] // STEP
    s_count = part // GROUP
    slots = SPLIT * part
    named = slots_ref[...]
    place = lax.broadcasted_iota(jnp.int32, named.shape, 0) % GROUP * s_count
    keys = named // s_count * part + place + named % s_count
    keys = jnp.where(named < SPLIT * s_count, keys, -1)
    row_ids = lax.broadcasted_iota(jnp.int32, (row_count, entries), 0)
    slot_ids = lax.broadcasted_iota(jnp.int32, (slots, entries), 0)
    lanes = lax.broadcasted_iota(jnp.int32, (part, EXTRA), 1)

    def side_by_side(values, step):
        first = step * GROUP
        return jnp.concatenate(
            [values[first + i : first + i + 1] for i in range(GROUP)], axis=1
        )

    for step in range(STEP):
        here = slice(step * part, (step + 1) * part)
        by_row = jnp.where(row_ids == side_by_side(rows_ref[...], step), 1.0, 0.0)
        hits = jnp.where(slot_ids == side_by_side(keys, step), 1.0, 0.0)
        chosen = contract_last(hits.astype(bf16), by_row.astype(bf16)).astype(bf16)
        count = jnp.sum(hits, axis=1, keepdims=True)
        tail = jnp.zeros((part, EXTRA), f32)
        for j in range(SPLIT):
            select_ref[j, here, :] = chosen[j * part : (j + 1) * part]
            tail = jnp.where(lanes == j, count[j * part : (j + 1) * part], tail)
        partial_ref[here, SPLIT * width :] = tail.astype(bf16)
    height = STEP * part
    chosen = select_ref[...].reshape(SPLIT * height, row_count)
    sums = jnp.dot(chosen, feats_ref[...], preferred_element_type=f32).astype(bf16)
    for j in range(SPLIT):
        partial_ref[:, j * width : (j + 1) * width] = sums[j * height : (j + 1) * height]


def select_and_sum(feats, edge_rows, edge_slots, slot_cap):
    dests, entry_cap = edge_rows.shape
    row_count, width = feats.shape
    s_count = slot_cap // SPLIT
    sent = dests * s_count
    steps = dests // (GROUP * STEP)
    wide = SPLIT * width + EXTRA
    edge_spec = pl.BlockSpec((GROUP * STEP, entry_cap), lambda i: (i, 0))
    return pl.pallas_call(
        select_kernel,
        grid=(steps,),
        in_specs=[
            edge_spec,
            edge_spec,
            pl.BlockSpec((row_count, width), lambda i: (0, 0)),
        ],
        out_specs=[
            pl.BlockSpec((SPLIT, sent // steps, row_count), lambda i: (0, i, 0)),
            pl.BlockSpec((sent // steps, wide), lambda i: (i, 0)),
        ],
        out_shape=[
            jax.ShapeDtypeStruct((SPLIT, sent, row_count), bf16),
            jax.ShapeDtypeStruct((sent, wide), bf16),
        ],
        compiler_params=VMEM,
        cost_estimate=cost(
            2 * SPLIT * sent * row_count * (width + GROUP * entry_cap),
            2 * (row_count * width + sent * (SPLIT * row_count + wide)),
        ),
    )(edge_rows, edge_slots, feats)


def middle_kernel(
    arrived_any,
    seeds_ref,
    base_any,
    w_neigh_any,
    cotangent_any,
    turned_any,
    self_any,
    hidden_any,
    delta_any,
    routed_any,
    terms_any,
    arrived_ref,
    base_ref,
    w_neigh_ref,
    cotangent_ref,
    turned_ref,
    self_ref,
    hidden_ref,
    delta_ref,
    routed_ref,
    terms_ref,
    aggregate_ref,
    neigh_ref,
    degree_ref,
    in_sems,
    out_sems,
):
    seed_count = base_ref.shape[0]
    width = w_neigh_ref.shape[0]
    sent = seeds_ref.shape[2]
    near, tall, hidden = terms_ref.shape
    block = tall - MARGIN
    ids = lax.broadcasted_iota(jnp.int32, (seed_count, sent), 0)
    lanes = lax.broadcasted_iota(jnp.int32, (seed_count, EXTRA), 1)

    def columns(j):
        return slice(j * width, (j + 1) * width if j < SPLIT else j * width + EXTRA)

    loads = []

    def load(source, target):
        copy = pltpu.make_async_copy(source, target, in_sems.at[len(loads)])
        copy.start()
        loads.append(copy)

    for j in (SPLIT, *range(SPLIT)):
        load(arrived_any.at[:, columns(j)], arrived_ref.at[:, columns(j)])
    load(w_neigh_any, w_neigh_ref)
    load(base_any, base_ref)
    load(cotangent_any, cotangent_ref)
    load(turned_any, turned_ref)
    load(self_any, self_ref)

    total = jnp.zeros((seed_count, width), f32)
    counts = jnp.zeros((seed_count, EXTRA), f32)
    loads[0].wait()
    for j in range(SPLIT):
        route = jnp.where(ids == seeds_ref[j], 1.0, 0.0).astype(bf16)
        loads[1 + j].wait()
        total += jnp.dot(route, arrived_ref[:, columns(j)], preferred_element_type=f32)
        found = jnp.dot(
            route, arrived_ref[:, columns(SPLIT)], preferred_element_type=f32
        )
        counts += jnp.where(lanes == j, found, 0.0)
    degree = jnp.maximum(jnp.sum(counts, axis=1, keepdims=True), 1.0)
    degree_ref[...] = jnp.broadcast_to(degree, (seed_count, EXTRA))
    aggregate_ref[...] = (total / degree).astype(bf16)
    for later in loads[1 + SPLIT :]:
        later.wait()
    base_ref[...] += jnp.dot(
        aggregate_ref[...], w_neigh_ref[...], preferred_element_type=f32
    )

    rows = 16
    slope = (2.0 / np.pi) ** 0.5

    @pl.loop(0, seed_count // rows)
    def _(i):
        here = pl.ds(pl.multiple_of(i * rows, rows), rows)
        pre = base_ref[here, :]
        square = pre * pre
        bend = jnp.tanh(slope * pre * (1.0 + 0.044715 * square))
        half = 0.5 * (1.0 + bend)
        hidden_ref[here, :] = (pre * half).astype(bf16)
        steep = half + 0.5 * pre * (1.0 - bend * bend) * (
            slope * (1.0 + 3 * 0.044715 * square)
        )
        delta = (cotangent_ref[here, :].astype(f32) * steep).astype(bf16)
        delta_ref[here, :] = delta
        neigh_ref[here, :] = (delta.astype(f32) / degree_ref[here, 0:1]).astype(bf16)

    copies = []

    def send(source, target):
        copy = pltpu.make_async_copy(source, target, out_sems.at[len(copies)])
        copy.start()
        copies.append(copy)

    grad = contract_last(neigh_ref[...], w_neigh_ref[...]).astype(bf16)
    for j in range(SPLIT):
        routed_ref[:, columns(j)] = jnp.dot(
            turned_ref[j], grad, preferred_element_type=f32
        ).astype(bf16)
        send(routed_ref.at[:, columns(j)], routed_any.at[:, columns(j)])

    send(hidden_ref, hidden_any)
    send(delta_ref, delta_any)
    delta = delta_ref[...]
    column = jnp.sum(delta.astype(f32), axis=0, keepdims=True)
    first = lax.broadcasted_iota(jnp.int32, (MARGIN, hidden), 0) == 0
    margin = jnp.where(first, column, 0.0).astype(bf16)
    half = near // 2
    products = (
        jnp.dot(self_ref[...], delta, preferred_element_type=f32),
        contract_first(aggregate_ref[...], delta),
    )
    for side, product in enumerate(products):
        product = product.astype(bf16)
        mine = slice(side * half, (side + 1) * half)
        for b in range(half):
            terms_ref[side * half + b, :block, :] = product[b * block : (b + 1) * block]
            terms_ref[side * half + b, block:, :] = margin
        send(terms_ref.at[mine], terms_any.at[mine])
    for copy in copies:
        copy.wait()


def middle(arrived, seeds, base, w_neigh, cotangent, turned, self_turned):
    sent, wide = arrived.shape
    seed_count, hidden = base.shape
    width = w_neigh.shape[0]
    near = lax.axis_size(NEAR)
    terms = (near, 2 * width // near + MARGIN, hidden)
    hbm = pl.BlockSpec(memory_space=pltpu.HBM)
    loaded = (arrived, base, w_neigh, cotangent, turned, self_turned)
    results = [
        jax.ShapeDtypeStruct((seed_count, hidden), bf16),
        jax.ShapeDtypeStruct((seed_count, hidden), bf16),
        jax.ShapeDtypeStruct((sent, SPLIT * width), bf16),
        jax.ShapeDtypeStruct(terms, bf16),
    ]
    return pl.pallas_call(
        middle_kernel,
        in_specs=[hbm, pl.BlockSpec(memory_space=pltpu.VMEM)] + [hbm] * 5,
        out_specs=[hbm] * 4,
        out_shape=results,
        scratch_shapes=[pltpu.VMEM(one.shape, one.dtype) for one in (*loaded, *results)]
        + [
            pltpu.VMEM((seed_count, width), bf16),
            pltpu.VMEM((seed_count, hidden), bf16),
            pltpu.VMEM((seed_count, EXTRA), f32),
            pltpu.SemaphoreType.DMA((SPLIT + 6,)),
            pltpu.SemaphoreType.DMA((SPLIT + 4,)),
        ],
        compiler_params=VMEM,
        cost_estimate=cost(
            4 * seed_count * width * (SPLIT * sent + 2 * hidden),
            2 * (2 * arrived.size + 3 * w_neigh.size + 5 * base.size),
        ),
    )(arrived, seeds, base, w_neigh, cotangent, turned, self_turned)


def after(value, earlier):
    def kernel(value_ref, earlier_ref, out_ref):
        pass

    return pl.pallas_call(
        kernel,
        in_specs=[pl.BlockSpec(memory_space=pl.ANY)] * 2,
        out_specs=pl.BlockSpec(memory_space=pl.ANY),
        out_shape=jax.ShapeDtypeStruct(value.shape, value.dtype),
        input_output_aliases={0: 0},
    )(value, earlier)


def reduce_everywhere(terms, earlier, meanwhile):
    _, tall, hidden = terms.shape
    block = tall - MARGIN
    part = block // lax.axis_size("x")
    summed = lax.psum_scatter(
        terms.reshape(-1, hidden), NEAR, scatter_dimension=0, tiled=True
    )
    parts = summed[:block].reshape(-1, part, hidden)
    margin = jnp.broadcast_to(summed[None, block:], (block // part, MARGIN, hidden))
    parts = jnp.concatenate([parts, margin], axis=1)
    line = lax.psum_scatter(
        parts.reshape(-1, hidden), "x", scatter_dimension=0, tiled=True
    )
    pieces = after(line, earlier[:1, :, :EXTRA]).reshape(lax.axis_size("z"), -1, hidden)
    total = jnp.sum(exchange(pieces, "z").astype(f32), axis=0).astype(bf16)
    own = exchange(spread(total, FAR), FAR).reshape(-1, part + MARGIN, hidden)
    own = jnp.concatenate([own[:, :part].reshape(block, hidden), own[0, part:]], axis=0)
    return lax.all_gather(after(own, meanwhile[:16, :EXTRA]), NEAR, axis=0, tiled=True)


def scaled_kernel(scale, upper_ref, lower_ref, self_ref, neigh_ref, bias_ref):
    block = self_ref.shape[0]
    self_ref[...] = upper_ref[:block, :].astype(f32) * scale
    neigh_ref[...] = lower_ref[:block, :].astype(f32) * scale

    @pl.when(pl.program_id(1) == 0)
    def _():
        bias_ref[...] = upper_ref[block : block + MARGIN, :].astype(f32)[0:1] * scale


def scaled_parts(full, width, scale):
    hidden = full.shape[1]
    near = lax.axis_size(NEAR)
    tall = full.shape[0] // near
    half = near // 2
    block = width // half
    pieces = 4
    piece = hidden // pieces
    grad_spec = pl.BlockSpec((block, piece), lambda c, i: (i, c))
    return pl.pallas_call(
        functools.partial(scaled_kernel, scale),
        grid=(pieces, half),
        in_specs=[
            pl.BlockSpec((tall, piece), lambda c, i: (i, c)),
            pl.BlockSpec((tall, piece), lambda c, i: (i + half, c)),
        ],
        out_specs=[
            grad_spec,
            grad_spec,
            pl.BlockSpec((1, piece), lambda c, i: (0, c)),
        ],
        out_shape=[
            jax.ShapeDtypeStruct((width, hidden), f32),
            jax.ShapeDtypeStruct((width, hidden), f32),
            jax.ShapeDtypeStruct((1, hidden), f32),
        ],
        compiler_params=VMEM,
        cost_estimate=cost(full.size, 6 * full.size),
    )(full, full)


def scatter_kernel(turned_any, grad_any, out_ref, turned_ref, grad_ref, sems):
    width = out_ref.shape[1]
    copies = []
    for j in range(SPLIT):
        columns = slice(j * width, (j + 1) * width)
        for k, (source, target) in enumerate(
            (
                (turned_any.at[j], turned_ref.at[j]),
                (grad_any.at[:, columns], grad_ref.at[:, columns]),
            )
        ):
            copy = pltpu.make_async_copy(source, target, sems.at[j, k])
            copy.start()
            copies.append(copy)
    total = jnp.zeros(out_ref.shape, f32)
    for j in range(SPLIT):
        copies[2 * j].wait()
        copies[2 * j + 1].wait()
        total += jnp.dot(
            turned_ref[j],
            grad_ref[:, j * width : (j + 1) * width],
            preferred_element_type=f32,
        )
    out_ref[...] = total.astype(bf16)


def scatter_sum(turned, slot_grad):
    _, rows, sent = turned.shape
    width = slot_grad.shape[1] // SPLIT
    return pl.pallas_call(
        scatter_kernel,
        in_specs=[pl.BlockSpec(memory_space=pltpu.HBM)] * 2,
        out_shape=jax.ShapeDtypeStruct((rows, width), bf16),
        scratch_shapes=[
            pltpu.VMEM(turned.shape, bf16),
            pltpu.VMEM(slot_grad.shape, bf16),
            pltpu.SemaphoreType.DMA((SPLIT, 2)),
        ],
        compiler_params=VMEM,
        cost_estimate=cost(
            2 * SPLIT * sent * rows * width, 2 * (turned.size + slot_grad.size)
        ),
    )(turned, slot_grad)


def on_device(
    feats, seed_rows, edge_rows, edge_slots, slot_seeds, w_self, w_neigh, bias, cotangent
):
    edge_rows = edge_rows[0]
    edge_slots = edge_slots[0]
    slot_seeds = slot_seeds[0]
    sources, slot_cap = slot_seeds.shape
    s_count = slot_cap // SPLIT
    seed_count = seed_rows.shape[0]
    width = feats.shape[1]
    replicas = lax.axis_size("rep")
    select, partial_value = select_and_sum(feats, edge_rows, edge_slots, slot_cap)
    arrived = exchange(partial_value.reshape(sources, s_count, -1), DOM)
    seeds = slot_seeds.reshape(sources, SPLIT, s_count).transpose(1, 0, 2)
    seeds = seeds.reshape(SPLIT, 1, sources * s_count)
    self_rows = jnp.take(feats, seed_rows, axis=0)
    base = jnp.dot(self_rows, w_self, preferred_element_type=f32) + bias[None, :]
    hidden_out, delta, routed, terms = middle(
        arrived.reshape(sources * s_count, -1),
        seeds,
        base,
        w_neigh,
        cotangent,
        (seeds.reshape(SPLIT, -1, 1) == jnp.arange(seed_count)).astype(bf16),
        self_rows.T,
    )

    slot_grad = exchange(routed.reshape(sources, s_count, -1), DOM)
    self_grad = contract_last(delta, w_self).astype(bf16)
    local = scatter_sum(jnp.swapaxes(select, 1, 2), slot_grad.reshape(sources * s_count, -1))
    feat_grads = lax.psum_scatter(local, "rep", scatter_dimension=0, tiled=True)
    full = reduce_everywhere(terms, slot_grad, feat_grads)
    scale = float(seed_count * lax.axis_size(DOM) * replicas) ** (-0.5)
    grad_self, grad_neigh, grad_bias = scaled_parts(full, width, scale)
    return (
        hidden_out,
        self_grad,
        feat_grads,
        grad_self,
        grad_neigh,
        grad_bias.reshape(-1),
    )


def solution(mesh):
    fine = Mesh(
        np.asarray(mesh.devices).reshape(8, 4, 2, 4), ("z", "x", "c", "rep")
    )
    every = DOM + ("rep",)
    in_specs = (
        P(DOM, None),
        P(every),
        P(every, None, None),
        P(every, None, None),
        P(every, None, None),
        P(),
        P(),
        P(),
        P(every, None),
    )
    out_specs = (P(every, None), P(every, None), P(every, None), P(), P(), P())
    return jax.shard_map(
        on_device, mesh=fine, in_specs=in_specs, out_specs=out_specs, check_vma=False
    )
```

```python
import functools

import jax
import jax.numpy as jnp
import numpy as np
from jax import lax
from jax.experimental import pallas as pl
from jax.experimental.pallas import tpu as pltpu
from jax.sharding import Mesh, PartitionSpec as P

DOM = ("z", "x", "c")
NEAR = ("c", "rep")
FAR = ("x", "z")
bf16 = jnp.bfloat16
f32 = jnp.float32

GROUP = 4
STEP = 4
SPLIT = 4
EXTRA = 128
VMEM = pltpu.CompilerParams(vmem_limit_bytes=60 * 1024 * 1024)
MARGIN = 16


def contract_first(left, right):
    return lax.dot_general(
        left, right, (((0,), (0,)), ((), ())), preferred_element_type=f32
    )


def contract_last(left, right):
    return lax.dot_general(
        left, right, (((1,), (1,)), ((), ())), preferred_element_type=f32
    )


def exchange(value, axes):
    return lax.all_to_all(value, axes, split_axis=0, concat_axis=0, tiled=True)


def spread(value, axes):
    return jnp.broadcast_to(value[None], (lax.axis_size(axes),) + value.shape)


def cost(flops, bytes_accessed):
    return pl.CostEstimate(flops=flops, bytes_accessed=bytes_accessed, transcendentals=0)


def select_kernel(rows_ref, slots_ref, feats_ref, select_ref, partial_ref):
    row_count, width = feats_ref.shape
    dests, entry_cap = rows_ref.shape
    entries = GROUP * entry_cap
    part = select_ref.shape[1] // STEP
    s_count = part // GROUP
    slots = SPLIT * part
    named = slots_ref[...]
    place = lax.broadcasted_iota(jnp.int32, named.shape, 0) % GROUP * s_count
    keys = named // s_count * part + place + named % s_count
    keys = jnp.where(named < SPLIT * s_count, keys, -1)
    row_ids = lax.broadcasted_iota(jnp.int32, (row_count, entries), 0)
    slot_ids = lax.broadcasted_iota(jnp.int32, (slots, entries), 0)
    lanes = lax.broadcasted_iota(jnp.int32, (part, EXTRA), 1)

    def side_by_side(values, step):
        first = step * GROUP
        return jnp.concatenate(
            [values[first + i : first + i + 1] for i in range(GROUP)], axis=1
        )

    for step in range(STEP):
        here = slice(step * part, (step + 1) * part)
        by_row = jnp.where(row_ids == side_by_side(rows_ref[...], step), 1.0, 0.0)
        hits = jnp.where(slot_ids == side_by_side(keys, step), 1.0, 0.0)
        chosen = contract_last(hits.astype(bf16), by_row.astype(bf16)).astype(bf16)
        count = jnp.sum(hits, axis=1, keepdims=True)
        tail = jnp.zeros((part, EXTRA), f32)
        for j in range(SPLIT):
            select_ref[j, here, :] = chosen[j * part : (j + 1) * part]
            tail = jnp.where(lanes == j, count[j * part : (j + 1) * part], tail)
        partial_ref[here, SPLIT * width :] = tail.astype(bf16)
    height = STEP * part
    chosen = select_ref[...].reshape(SPLIT * height, row_count)
    sums = jnp.dot(chosen, feats_ref[...], preferred_element_type=f32).astype(bf16)
    for j in range(SPLIT):
        partial_ref[:, j * width : (j + 1) * width] = sums[j * height : (j + 1) * height]


def select_and_sum(feats, edge_rows, edge_slots, slot_cap):
    dests, entry_cap = edge_rows.shape
    row_count, width = feats.shape
    s_count = slot_cap // SPLIT
    sent = dests * s_count
    steps = dests // (GROUP * STEP)
    wide = SPLIT * width + EXTRA
    edge_spec = pl.BlockSpec((GROUP * STEP, entry_cap), lambda i: (i, 0))
    return pl.pallas_call(
        select_kernel,
        grid=(steps,),
        in_specs=[
            edge_spec,
            edge_spec,
            pl.BlockSpec((row_count, width), lambda i: (0, 0)),
        ],
        out_specs=[
            pl.BlockSpec((SPLIT, sent // steps, row_count), lambda i: (0, i, 0)),
            pl.BlockSpec((sent // steps, wide), lambda i: (i, 0)),
        ],
        out_shape=[
            jax.ShapeDtypeStruct((SPLIT, sent, row_count), bf16),
            jax.ShapeDtypeStruct((sent, wide), bf16),
        ],
        compiler_params=VMEM,
        cost_estimate=cost(
            2 * SPLIT * sent * row_count * (width + GROUP * entry_cap),
            2 * (row_count * width + sent * (SPLIT * row_count + wide)),
        ),
    )(edge_rows, edge_slots, feats)


def middle_kernel(
    arrived_any,
    seeds_ref,
    base_any,
    w_neigh_any,
    cotangent_any,
    turned_any,
    self_any,
    hidden_any,
    delta_any,
    routed_any,
    terms_any,
    arrived_ref,
    base_ref,
    w_neigh_ref,
    cotangent_ref,
    turned_ref,
    self_ref,
    hidden_ref,
    delta_ref,
    routed_ref,
    terms_ref,
    aggregate_ref,
    neigh_ref,
    degree_ref,
    in_sems,
    out_sems,
):
    seed_count = base_ref.shape[0]
    width = w_neigh_ref.shape[0]
    sent = seeds_ref.shape[2]
    near, tall, hidden = terms_ref.shape
    block = tall - MARGIN
    ids = lax.broadcasted_iota(jnp.int32, (seed_count, sent), 0)
    lanes = lax.broadcasted_iota(jnp.int32, (seed_count, EXTRA), 1)

    def columns(j):
        return slice(j * width, (j + 1) * width if j < SPLIT else j * width + EXTRA)

    loads = []

    def load(source, target):
        copy = pltpu.make_async_copy(source, target, in_sems.at[len(loads)])
        copy.start()
        loads.append(copy)

    for j in (SPLIT, *range(SPLIT)):
        load(arrived_any.at[:, columns(j)], arrived_ref.at[:, columns(j)])
    load(w_neigh_any, w_neigh_ref)
    load(base_any, base_ref)
    load(cotangent_any, cotangent_ref)
    load(turned_any, turned_ref)
    load(self_any, self_ref)

    total = jnp.zeros((seed_count, width), f32)
    counts = jnp.zeros((seed_count, EXTRA), f32)
    loads[0].wait()
    for j in range(SPLIT):
        route = jnp.where(ids == seeds_ref[j], 1.0, 0.0).astype(bf16)
        loads[1 + j].wait()
        total += jnp.dot(route, arrived_ref[:, columns(j)], preferred_element_type=f32)
        found = jnp.dot(
            route, arrived_ref[:, columns(SPLIT)], preferred_element_type=f32
        )
        counts += jnp.where(lanes == j, found, 0.0)
    degree = jnp.maximum(jnp.sum(counts, axis=1, keepdims=True), 1.0)
    degree_ref[...] = jnp.broadcast_to(degree, (seed_count, EXTRA))
    aggregate_ref[...] = (total / degree).astype(bf16)
    for later in loads[1 + SPLIT :]:
        later.wait()
    base_ref[...] += jnp.dot(
        aggregate_ref[...], w_neigh_ref[...], preferred_element_type=f32
    )

    rows = 16
    slope = (2.0 / np.pi) ** 0.5

    @pl.loop(0, seed_count // rows)
    def _(i):
        here = pl.ds(pl.multiple_of(i * rows, rows), rows)
        pre = base_ref[here, :]
        square = pre * pre
        bend = jnp.tanh(slope * pre * (1.0 + 0.044715 * square))
        half = 0.5 * (1.0 + bend)
        hidden_ref[here, :] = (pre * half).astype(bf16)
        steep = half + 0.5 * pre * (1.0 - bend * bend) * (
            slope * (1.0 + 3 * 0.044715 * square)
        )
        delta = (cotangent_ref[here, :].astype(f32) * steep).astype(bf16)
        delta_ref[here, :] = delta
        neigh_ref[here, :] = (delta.astype(f32) / degree_ref[here, 0:1]).astype(bf16)

    copies = []

    def send(source, target):
        copy = pltpu.make_async_copy(source, target, out_sems.at[len(copies)])
        copy.start()
        copies.append(copy)

    grad = contract_last(neigh_ref[...], w_neigh_ref[...]).astype(bf16)
    for j in range(SPLIT):
        routed_ref[:, columns(j)] = jnp.dot(
            turned_ref[j], grad, preferred_element_type=f32
        ).astype(bf16)
        send(routed_ref.at[:, columns(j)], routed_any.at[:, columns(j)])

    send(hidden_ref, hidden_any)
    send(delta_ref, delta_any)
    delta = delta_ref[...]
    column = jnp.sum(delta.astype(f32), axis=0, keepdims=True)
    first = lax.broadcasted_iota(jnp.int32, (MARGIN, hidden), 0) == 0
    margin = jnp.where(first, column, 0.0).astype(bf16)
    half = near // 2
    products = (
        jnp.dot(self_ref[...], delta, preferred_element_type=f32),
        contract_first(aggregate_ref[...], delta),
    )
    for side, product in enumerate(products):
        product = product.astype(bf16)
        mine = slice(side * half, (side + 1) * half)
        for b in range(half):
            terms_ref[side * half + b, :block, :] = product[b * block : (b + 1) * block]
            terms_ref[side * half + b, block:, :] = margin
        send(terms_ref.at[mine], terms_any.at[mine])
    for copy in copies:
        copy.wait()


def middle(arrived, seeds, base, w_neigh, cotangent, turned, self_turned):
    sent, wide = arrived.shape
    seed_count, hidden = base.shape
    width = w_neigh.shape[0]
    near = lax.axis_size(NEAR)
    terms = (near, 2 * width // near + MARGIN, hidden)
    hbm = pl.BlockSpec(memory_space=pltpu.HBM)
    loaded = (arrived, base, w_neigh, cotangent, turned, self_turned)
    results = [
        jax.ShapeDtypeStruct((seed_count, hidden), bf16),
        jax.ShapeDtypeStruct((seed_count, hidden), bf16),
        jax.ShapeDtypeStruct((sent, SPLIT * width), bf16),
        jax.ShapeDtypeStruct(terms, bf16),
    ]
    return pl.pallas_call(
        middle_kernel,
        in_specs=[hbm, pl.BlockSpec(memory_space=pltpu.VMEM)] + [hbm] * 5,
        out_specs=[hbm] * 4,
        out_shape=results,
        scratch_shapes=[pltpu.VMEM(one.shape, one.dtype) for one in (*loaded, *results)]
        + [
            pltpu.VMEM((seed_count, width), bf16),
            pltpu.VMEM((seed_count, hidden), bf16),
            pltpu.VMEM((seed_count, EXTRA), f32),
            pltpu.SemaphoreType.DMA((SPLIT + 6,)),
            pltpu.SemaphoreType.DMA((SPLIT + 4,)),
        ],
        compiler_params=VMEM,
        cost_estimate=cost(
            4 * seed_count * width * (SPLIT * sent + 2 * hidden),
            2 * (2 * arrived.size + 3 * w_neigh.size + 5 * base.size),
        ),
    )(arrived, seeds, base, w_neigh, cotangent, turned, self_turned)


def after(value, earlier):
    def kernel(value_ref, earlier_ref, out_ref):
        pass

    return pl.pallas_call(
        kernel,
        in_specs=[pl.BlockSpec(memory_space=pl.ANY)] * 2,
        out_specs=pl.BlockSpec(memory_space=pl.ANY),
        out_shape=jax.ShapeDtypeStruct(value.shape, value.dtype),
        input_output_aliases={0: 0},
    )(value, earlier)


def reduce_everywhere(terms, earlier, meanwhile):
    _, tall, hidden = terms.shape
    block = tall - MARGIN
    part = block // lax.axis_size("x")
    summed = lax.psum_scatter(
        terms.reshape(-1, hidden), NEAR, scatter_dimension=0, tiled=True
    )
    parts = summed[:block].reshape(-1, part, hidden)
    margin = jnp.broadcast_to(summed[None, block:], (block // part, MARGIN, hidden))
    parts = jnp.concatenate([parts, margin], axis=1)
    line = lax.psum_scatter(
        parts.reshape(-1, hidden), "x", scatter_dimension=0, tiled=True
    )
    pieces = after(line, earlier).reshape(lax.axis_size("z"), -1, hidden)
    total = jnp.sum(exchange(pieces, "z").astype(f32), axis=0).astype(bf16)
    own = exchange(spread(total, FAR), FAR).reshape(-1, part + MARGIN, hidden)
    own = jnp.concatenate([own[:, :part].reshape(block, hidden), own[0, part:]], axis=0)
    return lax.all_gather(after(own, meanwhile), NEAR, axis=0, tiled=True)


def scaled_kernel(
    scale,
    full_any,
    self_any,
    neigh_any,
    bias_ref,
    full_ref,
    self_ref,
    neigh_ref,
    in_sems,
    out_sems,
):
    near, tall, _ = full_ref.shape
    half = near // 2
    block = tall - MARGIN
    order = [b for pair in zip(range(half), range(half, near)) for b in pair]
    loads, sends = {}, []
    for b in order:
        loads[b] = pltpu.make_async_copy(full_any.at[b], full_ref.at[b], in_sems.at[b])
        loads[b].start()
    for b in order:
        loads[b].wait()
        target, held = (self_any, self_ref) if b < half else (neigh_any, neigh_ref)
        here = slice(b % half * block, (b % half + 1) * block)
        held[here, :] = full_ref[b, :block, :].astype(f32) * scale
        copy = pltpu.make_async_copy(held.at[here], target.at[here], out_sems.at[b])
        copy.start()
        sends.append(copy)
    bias_ref[...] = full_ref[0, block:, :].astype(f32)[0:1] * scale
    for copy in sends:
        copy.wait()


def scaled_parts(full, width, scale):
    hidden = full.shape[1]
    near = lax.axis_size(NEAR)
    full = full.reshape(near, -1, hidden)
    grad = jax.ShapeDtypeStruct((width, hidden), f32)
    hbm = pl.BlockSpec(memory_space=pltpu.HBM)
    return pl.pallas_call(
        functools.partial(scaled_kernel, scale),
        in_specs=[hbm],
        out_specs=[hbm, hbm, pl.BlockSpec(memory_space=pltpu.VMEM)],
        out_shape=[grad, grad, jax.ShapeDtypeStruct((1, hidden), f32)],
        scratch_shapes=[
            pltpu.VMEM(full.shape, bf16),
            pltpu.VMEM(grad.shape, f32),
            pltpu.VMEM(grad.shape, f32),
            pltpu.SemaphoreType.DMA((near,)),
            pltpu.SemaphoreType.DMA((near,)),
        ],
        compiler_params=VMEM,
        cost_estimate=cost(full.size, 6 * full.size),
    )(full)


def scatter_kernel(
    turned_any, grad_any, out_ref, token_ref, turned_ref, grad_ref, sems
):
    width = out_ref.shape[1]
    copies = []
    for j in range(SPLIT):
        columns = slice(j * width, (j + 1) * width)
        for k, (source, target) in enumerate(
            (
                (turned_any.at[j], turned_ref.at[j]),
                (grad_any.at[:, columns], grad_ref.at[:, columns]),
            )
        ):
            copy = pltpu.make_async_copy(source, target, sems.at[j, k])
            copy.start()
            copies.append(copy)
    total = jnp.zeros(out_ref.shape, f32)
    for j in range(SPLIT):
        copies[2 * j].wait()
        copies[2 * j + 1].wait()
        total += jnp.dot(
            turned_ref[j],
            grad_ref[:, j * width : (j + 1) * width],
            preferred_element_type=f32,
        )
    out_ref[...] = total.astype(bf16)
    token_ref[...] = jnp.zeros(token_ref.shape, f32)


def scatter_sum(turned, slot_grad):
    _, rows, sent = turned.shape
    width = slot_grad.shape[1] // SPLIT
    return pl.pallas_call(
        scatter_kernel,
        in_specs=[pl.BlockSpec(memory_space=pltpu.HBM)] * 2,
        out_shape=[
            jax.ShapeDtypeStruct((rows, width), bf16),
            jax.ShapeDtypeStruct((8, EXTRA), f32),
        ],
        scratch_shapes=[
            pltpu.VMEM(turned.shape, bf16),
            pltpu.VMEM(slot_grad.shape, bf16),
            pltpu.SemaphoreType.DMA((SPLIT, 2)),
        ],
        compiler_params=VMEM,
        cost_estimate=cost(
            2 * SPLIT * sent * rows * width, 2 * (turned.size + slot_grad.size)
        ),
    )(turned, slot_grad)


def on_device(
    feats, seed_rows, edge_rows, edge_slots, slot_seeds, w_self, w_neigh, bias, cotangent
):
    edge_rows = edge_rows[0]
    edge_slots = edge_slots[0]
    slot_seeds = slot_seeds[0]
    sources, slot_cap = slot_seeds.shape
    s_count = slot_cap // SPLIT
    seed_count = seed_rows.shape[0]
    width = feats.shape[1]
    replicas = lax.axis_size("rep")
    select, partial_value = select_and_sum(feats, edge_rows, edge_slots, slot_cap)
    arrived = exchange(partial_value.reshape(sources, s_count, -1), DOM)
    seeds = slot_seeds.reshape(sources, SPLIT, s_count).transpose(1, 0, 2)
    seeds = seeds.reshape(SPLIT, 1, sources * s_count)
    self_rows = jnp.take(feats, seed_rows, axis=0)
    base = jnp.dot(self_rows, w_self, preferred_element_type=f32) + bias[None, :]
    hidden_out, delta, routed, terms = middle(
        arrived.reshape(sources * s_count, -1),
        seeds,
        base,
        w_neigh,
        cotangent,
        (seeds.reshape(SPLIT, -1, 1) == jnp.arange(seed_count)).astype(bf16),
        self_rows.T,
    )

    slot_grad = exchange(routed.reshape(sources, s_count, -1), DOM)
    self_grad = contract_last(delta, w_self).astype(bf16)
    local, summed = scatter_sum(
        jnp.swapaxes(select, 1, 2), slot_grad.reshape(sources * s_count, -1)
    )
    feat_grads = lax.psum_scatter(local, "rep", scatter_dimension=0, tiled=True)
    full = reduce_everywhere(terms, summed, feat_grads)
    scale = float(seed_count * lax.axis_size(DOM) * replicas) ** (-0.5)
    grad_self, grad_neigh, grad_bias = scaled_parts(full, width, scale)
    return (
        hidden_out,
        self_grad,
        feat_grads,
        grad_self,
        grad_neigh,
        grad_bias.reshape(-1),
    )


def solution(mesh):
    fine = Mesh(
        np.asarray(mesh.devices).reshape(8, 4, 2, 4), ("z", "x", "c", "rep")
    )
    every = DOM + ("rep",)
    in_specs = (
        P(DOM, None),
        P(every),
        P(every, None, None),
        P(every, None, None),
        P(every, None, None),
        P(),
        P(),
        P(),
        P(every, None),
    )
    out_specs = (P(every, None), P(every, None), P(every, None), P(), P(), P())
    return jax.shard_map(
        on_device, mesh=fine, in_specs=in_specs, out_specs=out_specs, check_vma=False
    )
```

```python
import functools

import jax
import jax.numpy as jnp
import numpy as np
from jax import lax
from jax.experimental import pallas as pl
from jax.experimental.pallas import tpu as pltpu
from jax.sharding import Mesh, PartitionSpec as P

DOM = ("z", "x", "c")
NEAR = ("c", "rep")
FAR = ("x", "z")
bf16 = jnp.bfloat16
f32 = jnp.float32

GROUP = 4
STEP = 4
SPLIT = 4
EXTRA = 128
VMEM = pltpu.CompilerParams(vmem_limit_bytes=60 * 1024 * 1024)
MARGIN = 16


def contract_first(left, right):
    return lax.dot_general(
        left, right, (((0,), (0,)), ((), ())), preferred_element_type=f32
    )


def contract_last(left, right):
    return lax.dot_general(
        left, right, (((1,), (1,)), ((), ())), preferred_element_type=f32
    )


def exchange(value, axes):
    return lax.all_to_all(value, axes, split_axis=0, concat_axis=0, tiled=True)


def spread(value, axes):
    return jnp.broadcast_to(value[None], (lax.axis_size(axes),) + value.shape)


def cost(flops, bytes_accessed):
    return pl.CostEstimate(flops=flops, bytes_accessed=bytes_accessed, transcendentals=0)


def select_kernel(rows_ref, slots_ref, feats_ref, select_ref, partial_ref):
    row_count, width = feats_ref.shape
    dests, entry_cap = rows_ref.shape
    entries = GROUP * entry_cap
    part = select_ref.shape[1] // STEP
    s_count = part // GROUP
    slots = SPLIT * part
    named = slots_ref[...]
    place = lax.broadcasted_iota(jnp.int32, named.shape, 0) % GROUP * s_count
    keys = named // s_count * part + place + named % s_count
    keys = jnp.where(named < SPLIT * s_count, keys, -1)
    row_ids = lax.broadcasted_iota(jnp.int32, (row_count, entries), 0)
    slot_ids = lax.broadcasted_iota(jnp.int32, (slots, entries), 0)
    lanes = lax.broadcasted_iota(jnp.int32, (part, EXTRA), 1)

    def side_by_side(values, step):
        first = step * GROUP
        return jnp.concatenate(
            [values[first + i : first + i + 1] for i in range(GROUP)], axis=1
        )

    for step in range(STEP):
        here = slice(step * part, (step + 1) * part)
        by_row = jnp.where(row_ids == side_by_side(rows_ref[...], step), 1.0, 0.0)
        hits = jnp.where(slot_ids == side_by_side(keys, step), 1.0, 0.0)
        chosen = contract_last(hits.astype(bf16), by_row.astype(bf16)).astype(bf16)
        count = jnp.sum(hits, axis=1, keepdims=True)
        tail = jnp.zeros((part, EXTRA), f32)
        for j in range(SPLIT):
            select_ref[j, here, :] = chosen[j * part : (j + 1) * part]
            tail = jnp.where(lanes == j, count[j * part : (j + 1) * part], tail)
        partial_ref[here, SPLIT * width :] = tail.astype(bf16)
    height = STEP * part
    chosen = select_ref[...].reshape(SPLIT * height, row_count)
    sums = jnp.dot(chosen, feats_ref[...], preferred_element_type=f32).astype(bf16)
    for j in range(SPLIT):
        partial_ref[:, j * width : (j + 1) * width] = sums[j * height : (j + 1) * height]


def select_and_sum(feats, edge_rows, edge_slots, slot_cap):
    dests, entry_cap = edge_rows.shape
    row_count, width = feats.shape
    s_count = slot_cap // SPLIT
    sent = dests * s_count
    steps = dests // (GROUP * STEP)
    wide = SPLIT * width + EXTRA
    edge_spec = pl.BlockSpec((GROUP * STEP, entry_cap), lambda i: (i, 0))
    return pl.pallas_call(
        select_kernel,
        grid=(steps,),
        in_specs=[
            edge_spec,
            edge_spec,
            pl.BlockSpec((row_count, width), lambda i: (0, 0)),
        ],
        out_specs=[
            pl.BlockSpec((SPLIT, sent // steps, row_count), lambda i: (0, i, 0)),
            pl.BlockSpec((sent // steps, wide), lambda i: (i, 0)),
        ],
        out_shape=[
            jax.ShapeDtypeStruct((SPLIT, sent, row_count), bf16),
            jax.ShapeDtypeStruct((sent, wide), bf16),
        ],
        compiler_params=VMEM,
        cost_estimate=cost(
            2 * SPLIT * sent * row_count * (width + GROUP * entry_cap),
            2 * (row_count * width + sent * (SPLIT * row_count + wide)),
        ),
    )(edge_rows, edge_slots, feats)


def middle_kernel(
    arrived_any,
    seeds_ref,
    base_any,
    w_neigh_any,
    cotangent_any,
    turned_any,
    self_any,
    hidden_any,
    delta_any,
    routed_any,
    terms_any,
    arrived_ref,
    base_ref,
    w_neigh_ref,
    cotangent_ref,
    turned_ref,
    self_ref,
    hidden_ref,
    delta_ref,
    routed_ref,
    terms_ref,
    aggregate_ref,
    neigh_ref,
    degree_ref,
    in_sems,
    out_sems,
):
    seed_count = base_ref.shape[0]
    width = w_neigh_ref.shape[0]
    sent = seeds_ref.shape[2]
    near, tall, hidden = terms_ref.shape
    block = tall - MARGIN
    ids = lax.broadcasted_iota(jnp.int32, (seed_count, sent), 0)
    lanes = lax.broadcasted_iota(jnp.int32, (seed_count, EXTRA), 1)

    def columns(j):
        return slice(j * width, (j + 1) * width if j < SPLIT else j * width + EXTRA)

    loads = []

    def load(source, target):
        copy = pltpu.make_async_copy(source, target, in_sems.at[len(loads)])
        copy.start()
        loads.append(copy)

    for j in (SPLIT, *range(SPLIT)):
        load(arrived_any.at[:, columns(j)], arrived_ref.at[:, columns(j)])
    load(w_neigh_any, w_neigh_ref)
    load(base_any, base_ref)
    load(cotangent_any, cotangent_ref)
    load(turned_any, turned_ref)
    load(self_any, self_ref)

    total = jnp.zeros((seed_count, width), f32)
    counts = jnp.zeros((seed_count, EXTRA), f32)
    loads[0].wait()
    for j in range(SPLIT):
        route = jnp.where(ids == seeds_ref[j], 1.0, 0.0).astype(bf16)
        loads[1 + j].wait()
        total += jnp.dot(route, arrived_ref[:, columns(j)], preferred_element_type=f32)
        found = jnp.dot(
            route, arrived_ref[:, columns(SPLIT)], preferred_element_type=f32
        )
        counts += jnp.where(lanes == j, found, 0.0)
    degree = jnp.maximum(jnp.sum(counts, axis=1, keepdims=True), 1.0)
    degree_ref[...] = jnp.broadcast_to(degree, (seed_count, EXTRA))
    aggregate_ref[...] = (total / degree).astype(bf16)
    w_neigh_load, base_load, cotangent_load, turned_load, self_load = loads[1 + SPLIT :]
    w_neigh_load.wait()
    base_load.wait()
    base_ref[...] += jnp.dot(
        aggregate_ref[...], w_neigh_ref[...], preferred_element_type=f32
    )

    cotangent_load.wait()
    rows = 16
    slope = (2.0 / np.pi) ** 0.5

    @pl.loop(0, seed_count // rows)
    def _(i):
        here = pl.ds(pl.multiple_of(i * rows, rows), rows)
        pre = base_ref[here, :]
        square = pre * pre
        bend = jnp.tanh(slope * pre * (1.0 + 0.044715 * square))
        half = 0.5 * (1.0 + bend)
        hidden_ref[here, :] = (pre * half).astype(bf16)
        steep = half + 0.5 * pre * (1.0 - bend * bend) * (
            slope * (1.0 + 3 * 0.044715 * square)
        )
        delta = (cotangent_ref[here, :].astype(f32) * steep).astype(bf16)
        delta_ref[here, :] = delta
        neigh_ref[here, :] = (delta.astype(f32) / degree_ref[here, 0:1]).astype(bf16)

    copies = []

    def send(source, target):
        copy = pltpu.make_async_copy(source, target, out_sems.at[len(copies)])
        copy.start()
        copies.append(copy)

    grad = contract_last(neigh_ref[...], w_neigh_ref[...]).astype(bf16)
    turned_load.wait()
    for j in range(SPLIT):
        routed_ref[:, columns(j)] = jnp.dot(
            turned_ref[j], grad, preferred_element_type=f32
        ).astype(bf16)
        send(routed_ref.at[:, columns(j)], routed_any.at[:, columns(j)])

    send(hidden_ref, hidden_any)
    send(delta_ref, delta_any)
    delta = delta_ref[...]
    column = jnp.sum(delta.astype(f32), axis=0, keepdims=True)
    first = lax.broadcasted_iota(jnp.int32, (MARGIN, hidden), 0) == 0
    margin = jnp.where(first, column, 0.0).astype(bf16)
    half = near // 2
    self_load.wait()
    products = (
        jnp.dot(self_ref[...], delta, preferred_element_type=f32),
        contract_first(aggregate_ref[...], delta),
    )
    for side, product in enumerate(products):
        product = product.astype(bf16)
        mine = slice(side * half, (side + 1) * half)
        for b in range(half):
            terms_ref[side * half + b, :block, :] = product[b * block : (b + 1) * block]
            terms_ref[side * half + b, block:, :] = margin
        send(terms_ref.at[mine], terms_any.at[mine])
    for copy in copies:
        copy.wait()


def middle(arrived, seeds, base, w_neigh, cotangent, turned, self_turned):
    sent, wide = arrived.shape
    seed_count, hidden = base.shape
    width = w_neigh.shape[0]
    near = lax.axis_size(NEAR)
    terms = (near, 2 * width // near + MARGIN, hidden)
    hbm = pl.BlockSpec(memory_space=pltpu.HBM)
    loaded = (arrived, base, w_neigh, cotangent, turned, self_turned)
    results = [
        jax.ShapeDtypeStruct((seed_count, hidden), bf16),
        jax.ShapeDtypeStruct((seed_count, hidden), bf16),
        jax.ShapeDtypeStruct((sent, SPLIT * width), bf16),
        jax.ShapeDtypeStruct(terms, bf16),
    ]
    return pl.pallas_call(
        middle_kernel,
        in_specs=[hbm, pl.BlockSpec(memory_space=pltpu.VMEM)] + [hbm] * 5,
        out_specs=[hbm] * 4,
        out_shape=results,
        scratch_shapes=[pltpu.VMEM(one.shape, one.dtype) for one in (*loaded, *results)]
        + [
            pltpu.VMEM((seed_count, width), bf16),
            pltpu.VMEM((seed_count, hidden), bf16),
            pltpu.VMEM((seed_count, EXTRA), f32),
            pltpu.SemaphoreType.DMA((SPLIT + 6,)),
            pltpu.SemaphoreType.DMA((SPLIT + 4,)),
        ],
        compiler_params=VMEM,
        cost_estimate=cost(
            4 * seed_count * width * (SPLIT * sent + 2 * hidden),
            2 * (2 * arrived.size + 3 * w_neigh.size + 5 * base.size),
        ),
    )(arrived, seeds, base, w_neigh, cotangent, turned, self_turned)


def after(value, earlier):
    def kernel(value_ref, earlier_ref, out_ref):
        pass

    return pl.pallas_call(
        kernel,
        in_specs=[pl.BlockSpec(memory_space=pl.ANY)] * 2,
        out_specs=pl.BlockSpec(memory_space=pl.ANY),
        out_shape=jax.ShapeDtypeStruct(value.shape, value.dtype),
        input_output_aliases={0: 0},
    )(value, earlier)


def reduce_everywhere(terms, earlier, meanwhile):
    _, tall, hidden = terms.shape
    block = tall - MARGIN
    part = block // lax.axis_size("x")
    summed = lax.psum_scatter(
        terms.reshape(-1, hidden), NEAR, scatter_dimension=0, tiled=True
    )
    parts = summed[:block].reshape(-1, part, hidden)
    margin = jnp.broadcast_to(summed[None, block:], (block // part, MARGIN, hidden))
    parts = jnp.concatenate([parts, margin], axis=1)
    line = lax.psum_scatter(
        parts.reshape(-1, hidden), "x", scatter_dimension=0, tiled=True
    )
    pieces = after(line, earlier).reshape(lax.axis_size("z"), -1, hidden)
    total = jnp.sum(exchange(pieces, "z").astype(f32), axis=0).astype(bf16)
    own = exchange(spread(total, FAR), FAR).reshape(-1, part + MARGIN, hidden)
    own = jnp.concatenate([own[:, :part].reshape(block, hidden), own[0, part:]], axis=0)
    return lax.all_gather(after(own, meanwhile), NEAR, axis=0, tiled=True)


def scaled_kernel(
    scale,
    full_any,
    self_any,
    neigh_any,
    bias_ref,
    full_ref,
    self_ref,
    neigh_ref,
    in_sems,
    out_sems,
):
    near, tall, _ = full_ref.shape
    half = near // 2
    block = tall - MARGIN
    order = [b for pair in zip(range(half), range(half, near)) for b in pair]
    loads, sends = {}, []
    for b in order:
        loads[b] = pltpu.make_async_copy(full_any.at[b], full_ref.at[b], in_sems.at[b])
        loads[b].start()
    for b in order:
        loads[b].wait()
        target, held = (self_any, self_ref) if b < half else (neigh_any, neigh_ref)
        here = slice(b % half * block, (b % half + 1) * block)
        held[here, :] = full_ref[b, :block, :].astype(f32) * scale
        copy = pltpu.make_async_copy(held.at[here], target.at[here], out_sems.at[b])
        copy.start()
        sends.append(copy)
    bias_ref[...] = full_ref[0, block:, :].astype(f32)[0:1] * scale
    for copy in sends:
        copy.wait()


def scaled_parts(full, width, scale):
    hidden = full.shape[1]
    near = lax.axis_size(NEAR)
    full = full.reshape(near, -1, hidden)
    grad = jax.ShapeDtypeStruct((width, hidden), f32)
    hbm = pl.BlockSpec(memory_space=pltpu.HBM)
    return pl.pallas_call(
        functools.partial(scaled_kernel, scale),
        in_specs=[hbm],
        out_specs=[hbm, hbm, pl.BlockSpec(memory_space=pltpu.VMEM)],
        out_shape=[grad, grad, jax.ShapeDtypeStruct((1, hidden), f32)],
        scratch_shapes=[
            pltpu.VMEM(full.shape, bf16),
            pltpu.VMEM(grad.shape, f32),
            pltpu.VMEM(grad.shape, f32),
            pltpu.SemaphoreType.DMA((near,)),
            pltpu.SemaphoreType.DMA((near,)),
        ],
        compiler_params=VMEM,
        cost_estimate=cost(full.size, 6 * full.size),
    )(full)


def scatter_kernel(turned_ref, grad_ref, out_ref, token_ref):
    width = out_ref.shape[1]
    total = jnp.zeros(out_ref.shape, f32)
    for j in range(SPLIT):
        total += jnp.dot(
            turned_ref[j],
            grad_ref[:, j * width : (j + 1) * width],
            preferred_element_type=f32,
        )
    out_ref[...] = total.astype(bf16)
    token_ref[...] = jnp.zeros(token_ref.shape, f32)


def scatter_sum(turned, slot_grad):
    _, rows, sent = turned.shape
    width = slot_grad.shape[1] // SPLIT
    return pl.pallas_call(
        scatter_kernel,
        out_shape=[
            jax.ShapeDtypeStruct((rows, width), bf16),
            jax.ShapeDtypeStruct((8, EXTRA), f32),
        ],
        compiler_params=pltpu.CompilerParams(vmem_limit_bytes=32 * 1024 * 1024),
        cost_estimate=cost(
            2 * SPLIT * sent * rows * width, 2 * (turned.size + slot_grad.size)
        ),
    )(turned, slot_grad)


def on_device(
    feats, seed_rows, edge_rows, edge_slots, slot_seeds, w_self, w_neigh, bias, cotangent
):
    edge_rows = edge_rows[0]
    edge_slots = edge_slots[0]
    slot_seeds = slot_seeds[0]
    sources, slot_cap = slot_seeds.shape
    s_count = slot_cap // SPLIT
    seed_count = seed_rows.shape[0]
    width = feats.shape[1]
    replicas = lax.axis_size("rep")
    select, partial_value = select_and_sum(feats, edge_rows, edge_slots, slot_cap)
    arrived = exchange(partial_value.reshape(sources, s_count, -1), DOM)
    seeds = slot_seeds.reshape(sources, SPLIT, s_count).transpose(1, 0, 2)
    seeds = seeds.reshape(SPLIT, 1, sources * s_count)
    self_rows = jnp.take(feats, seed_rows, axis=0)
    base = jnp.dot(self_rows, w_self, preferred_element_type=f32) + bias[None, :]
    hidden_out, delta, routed, terms = middle(
        arrived.reshape(sources * s_count, -1),
        seeds,
        base,
        w_neigh,
        cotangent,
        (seeds.reshape(SPLIT, -1, 1) == jnp.arange(seed_count)).astype(bf16),
        self_rows.T,
    )

    slot_grad = exchange(routed.reshape(sources, s_count, -1), DOM)
    self_grad = contract_last(delta, w_self).astype(bf16)
    local, summed = scatter_sum(
        jnp.swapaxes(select, 1, 2), slot_grad.reshape(sources * s_count, -1)
    )
    feat_grads = lax.psum_scatter(local, "rep", scatter_dimension=0, tiled=True)
    full = reduce_everywhere(terms, summed, feat_grads)
    scale = float(seed_count * lax.axis_size(DOM) * replicas) ** (-0.5)
    grad_self, grad_neigh, grad_bias = scaled_parts(full, width, scale)
    return (
        hidden_out,
        self_grad,
        feat_grads,
        grad_self,
        grad_neigh,
        grad_bias.reshape(-1),
    )


def solution(mesh):
    fine = Mesh(
        np.asarray(mesh.devices).reshape(8, 4, 2, 4), ("z", "x", "c", "rep")
    )
    every = DOM + ("rep",)
    in_specs = (
        P(DOM, None),
        P(every),
        P(every, None, None),
        P(every, None, None),
        P(every, None, None),
        P(),
        P(),
        P(),
        P(every, None),
    )
    out_specs = (P(every, None), P(every, None), P(every, None), P(), P(), P())
    return jax.shard_map(
        on_device, mesh=fine, in_specs=in_specs, out_specs=out_specs, check_vma=False
    )
```

```python
import functools

import jax
import jax.numpy as jnp
import numpy as np
from jax import lax
from jax.experimental import pallas as pl
from jax.experimental.pallas import tpu as pltpu
from jax.sharding import Mesh, PartitionSpec as P

DOM = ("z", "x", "c")
NEAR = ("c", "rep")
bf16 = jnp.bfloat16
f32 = jnp.float32

GROUP = 4
STEP = 4
SPLIT = 4
EXTRA = 128
VMEM = pltpu.CompilerParams(vmem_limit_bytes=60 * 1024 * 1024)
MARGIN = 16


def contract_first(left, right):
    return lax.dot_general(
        left, right, (((0,), (0,)), ((), ())), preferred_element_type=f32
    )


def contract_last(left, right):
    return lax.dot_general(
        left, right, (((1,), (1,)), ((), ())), preferred_element_type=f32
    )


def exchange(value, axes):
    return lax.all_to_all(value, axes, split_axis=0, concat_axis=0, tiled=True)


def spread(value, axes):
    return jnp.broadcast_to(value[None], (lax.axis_size(axes),) + value.shape)


def cost(flops, bytes_accessed):
    return pl.CostEstimate(flops=flops, bytes_accessed=bytes_accessed, transcendentals=0)


def select_kernel(
    rows_ref, slots_ref, feats_any, select_ref, partial_ref, feats_ref, feats_sem
):
    feats_load = pltpu.make_async_copy(feats_any, feats_ref, feats_sem)

    @pl.when(pl.program_id(0) == 0)
    def _():
        feats_load.start()

    row_count, width = feats_ref.shape
    dests, entry_cap = rows_ref.shape
    entries = GROUP * entry_cap
    part = select_ref.shape[1] // STEP
    s_count = part // GROUP
    slots = SPLIT * part
    named = slots_ref[...]
    place = lax.broadcasted_iota(jnp.int32, named.shape, 0) % GROUP * s_count
    keys = named // s_count * part + place + named % s_count
    keys = jnp.where(named < SPLIT * s_count, keys, -1)
    row_ids = lax.broadcasted_iota(jnp.int32, (row_count, entries), 0)
    slot_ids = lax.broadcasted_iota(jnp.int32, (slots, entries), 0)
    lanes = lax.broadcasted_iota(jnp.int32, (part, EXTRA), 1)

    def side_by_side(values, step):
        first = step * GROUP
        return jnp.concatenate(
            [values[first + i : first + i + 1] for i in range(GROUP)], axis=1
        )

    for step in range(STEP):
        here = slice(step * part, (step + 1) * part)
        by_row = jnp.where(row_ids == side_by_side(rows_ref[...], step), 1.0, 0.0)
        hits = jnp.where(slot_ids == side_by_side(keys, step), 1.0, 0.0)
        chosen = contract_last(hits.astype(bf16), by_row.astype(bf16)).astype(bf16)
        count = jnp.sum(hits, axis=1, keepdims=True)
        tail = jnp.zeros((part, EXTRA), f32)
        for j in range(SPLIT):
            select_ref[j, here, :] = chosen[j * part : (j + 1) * part]
            tail = jnp.where(lanes == j, count[j * part : (j + 1) * part], tail)
        partial_ref[here, SPLIT * width :] = tail.astype(bf16)
    @pl.when(pl.program_id(0) == 0)
    def _():
        feats_load.wait()

    height = STEP * part
    chosen = select_ref[...].reshape(SPLIT * height, row_count)
    sums = jnp.dot(chosen, feats_ref[...], preferred_element_type=f32).astype(bf16)
    for j in range(SPLIT):
        partial_ref[:, j * width : (j + 1) * width] = sums[j * height : (j + 1) * height]


def select_and_sum(feats, edge_rows, edge_slots, slot_cap):
    dests, entry_cap = edge_rows.shape
    row_count, width = feats.shape
    s_count = slot_cap // SPLIT
    sent = dests * s_count
    steps = dests // (GROUP * STEP)
    wide = SPLIT * width + EXTRA
    edge_spec = pl.BlockSpec((GROUP * STEP, entry_cap), lambda i: (i, 0))
    return pl.pallas_call(
        select_kernel,
        grid=(steps,),
        in_specs=[
            edge_spec,
            edge_spec,
            pl.BlockSpec(memory_space=pltpu.HBM),
        ],
        out_specs=[
            pl.BlockSpec((SPLIT, sent // steps, row_count), lambda i: (0, i, 0)),
            pl.BlockSpec((sent // steps, wide), lambda i: (i, 0)),
        ],
        out_shape=[
            jax.ShapeDtypeStruct((SPLIT, sent, row_count), bf16),
            jax.ShapeDtypeStruct((sent, wide), bf16),
        ],
        scratch_shapes=[
            pltpu.VMEM((row_count, width), bf16),
            pltpu.SemaphoreType.DMA,
        ],
        compiler_params=VMEM,
        cost_estimate=cost(
            2 * SPLIT * sent * row_count * (width + GROUP * entry_cap),
            2 * (row_count * width + sent * (SPLIT * row_count + wide)),
        ),
    )(edge_rows, edge_slots, feats)


def middle_kernel(
    arrived_any,
    seeds_ref,
    base_any,
    w_neigh_any,
    cotangent_any,
    turned_any,
    self_any,
    hidden_any,
    delta_any,
    routed_any,
    terms_any,
    arrived_ref,
    base_ref,
    w_neigh_ref,
    cotangent_ref,
    turned_ref,
    self_ref,
    hidden_ref,
    delta_ref,
    routed_ref,
    terms_ref,
    aggregate_ref,
    neigh_ref,
    degree_ref,
    in_sems,
    out_sems,
):
    seed_count = base_ref.shape[0]
    width = w_neigh_ref.shape[0]
    sent = seeds_ref.shape[2]
    near, tall, hidden = terms_ref.shape
    block = tall - MARGIN
    ids = lax.broadcasted_iota(jnp.int32, (seed_count, sent), 0)
    lanes = lax.broadcasted_iota(jnp.int32, (seed_count, EXTRA), 1)

    def columns(j):
        return slice(j * width, (j + 1) * width if j < SPLIT else j * width + EXTRA)

    loads = []

    def load(source, target):
        copy = pltpu.make_async_copy(source, target, in_sems.at[len(loads)])
        copy.start()
        loads.append(copy)

    for j in (SPLIT, *range(SPLIT)):
        load(arrived_any.at[:, columns(j)], arrived_ref.at[:, columns(j)])
    load(w_neigh_any, w_neigh_ref)
    load(base_any, base_ref)
    load(cotangent_any, cotangent_ref)
    load(turned_any, turned_ref)
    load(self_any, self_ref)

    total = jnp.zeros((seed_count, width), f32)
    counts = jnp.zeros((seed_count, EXTRA), f32)
    loads[0].wait()
    for j in range(SPLIT):
        route = jnp.where(ids == seeds_ref[j], 1.0, 0.0).astype(bf16)
        loads[1 + j].wait()
        total += jnp.dot(route, arrived_ref[:, columns(j)], preferred_element_type=f32)
        found = jnp.dot(
            route, arrived_ref[:, columns(SPLIT)], preferred_element_type=f32
        )
        counts += jnp.where(lanes == j, found, 0.0)
    degree = jnp.maximum(jnp.sum(counts, axis=1, keepdims=True), 1.0)
    degree_ref[...] = jnp.broadcast_to(degree, (seed_count, EXTRA))
    aggregate_ref[...] = (total / degree).astype(bf16)
    for later in loads[1 + SPLIT :]:
        later.wait()
    base_ref[...] += jnp.dot(
        aggregate_ref[...], w_neigh_ref[...], preferred_element_type=f32
    )

    rows = 16
    slope = (2.0 / np.pi) ** 0.5

    @pl.loop(0, seed_count // rows)
    def _(i):
        here = pl.ds(pl.multiple_of(i * rows, rows), rows)
        pre = base_ref[here, :]
        square = pre * pre
        bend = jnp.tanh(slope * pre * (1.0 + 0.044715 * square))
        half = 0.5 * (1.0 + bend)
        hidden_ref[here, :] = (pre * half).astype(bf16)
        steep = half + 0.5 * pre * (1.0 - bend * bend) * (
            slope * (1.0 + 3 * 0.044715 * square)
        )
        delta = (cotangent_ref[here, :].astype(f32) * steep).astype(bf16)
        delta_ref[here, :] = delta
        neigh_ref[here, :] = (delta.astype(f32) / degree_ref[here, 0:1]).astype(bf16)

    copies = []

    def send(source, target):
        copy = pltpu.make_async_copy(source, target, out_sems.at[len(copies)])
        copy.start()
        copies.append(copy)

    send(hidden_ref, hidden_any)
    send(delta_ref, delta_any)
    grad = contract_last(neigh_ref[...], w_neigh_ref[...]).astype(bf16)
    for j in range(SPLIT):
        routed_ref[:, columns(j)] = jnp.dot(
            turned_ref[j], grad, preferred_element_type=f32
        ).astype(bf16)
        send(routed_ref.at[:, columns(j)], routed_any.at[:, columns(j)])

    delta = delta_ref[...]
    column = jnp.sum(delta.astype(f32), axis=0, keepdims=True)
    first = lax.broadcasted_iota(jnp.int32, (MARGIN, hidden), 0) == 0
    margin = jnp.where(first, column, 0.0).astype(bf16)
    half = near // 2
    products = (
        jnp.dot(self_ref[...], delta, preferred_element_type=f32),
        contract_first(aggregate_ref[...], delta),
    )
    for side, product in enumerate(products):
        product = product.astype(bf16)
        mine = slice(side * half, (side + 1) * half)
        for b in range(half):
            terms_ref[side * half + b, :block, :] = product[b * block : (b + 1) * block]
            terms_ref[side * half + b, block:, :] = margin
        send(terms_ref.at[mine], terms_any.at[mine])
    for copy in copies:
        copy.wait()


def middle(arrived, seeds, base, w_neigh, cotangent, turned, self_turned):
    sent, wide = arrived.shape
    seed_count, hidden = base.shape
    width = w_neigh.shape[0]
    near = lax.axis_size(NEAR)
    terms = (near, 2 * width // near + MARGIN, hidden)
    hbm = pl.BlockSpec(memory_space=pltpu.HBM)
    loaded = (arrived, base, w_neigh, cotangent, turned, self_turned)
    results = [
        jax.ShapeDtypeStruct((seed_count, hidden), bf16),
        jax.ShapeDtypeStruct((seed_count, hidden), bf16),
        jax.ShapeDtypeStruct((sent, SPLIT * width), bf16),
        jax.ShapeDtypeStruct(terms, bf16),
    ]
    return pl.pallas_call(
        middle_kernel,
        in_specs=[hbm, pl.BlockSpec(memory_space=pltpu.VMEM)] + [hbm] * 5,
        out_specs=[hbm] * 4,
        out_shape=results,
        scratch_shapes=[pltpu.VMEM(one.shape, one.dtype) for one in (*loaded, *results)]
        + [
            pltpu.VMEM((seed_count, width), bf16),
            pltpu.VMEM((seed_count, hidden), bf16),
            pltpu.VMEM((seed_count, EXTRA), f32),
            pltpu.SemaphoreType.DMA((SPLIT + 6,)),
            pltpu.SemaphoreType.DMA((SPLIT + 4,)),
        ],
        compiler_params=VMEM,
        cost_estimate=cost(
            4 * seed_count * width * (SPLIT * sent + 2 * hidden),
            2 * (2 * arrived.size + 3 * w_neigh.size + 5 * base.size),
        ),
    )(arrived, seeds, base, w_neigh, cotangent, turned, self_turned)


def after(value, earlier):
    def kernel(value_ref, earlier_ref, out_ref):
        pass

    return pl.pallas_call(
        kernel,
        in_specs=[pl.BlockSpec(memory_space=pl.ANY)] * 2,
        out_specs=pl.BlockSpec(memory_space=pl.ANY),
        out_shape=jax.ShapeDtypeStruct(value.shape, value.dtype),
        input_output_aliases={0: 0},
    )(value, earlier)


def reduce_everywhere(terms, earlier, meanwhile):
    _, tall, hidden = terms.shape
    block = tall - MARGIN
    height = lax.axis_size("z")
    part = block // height
    summed = lax.psum_scatter(
        terms.reshape(-1, hidden), NEAR, scatter_dimension=0, tiled=True
    )
    parts = summed[:block].reshape(height, part, hidden)
    margin = jnp.broadcast_to(summed[None, block : block + 8], (height, 8, hidden))
    parts = jnp.concatenate([parts, margin], axis=1)
    line = lax.psum_scatter(
        parts.reshape(-1, hidden), "z", scatter_dimension=0, tiled=True
    )
    lines = exchange(spread(after(line, earlier), "x"), "x")
    total = jnp.sum(lines.astype(f32), axis=0).astype(bf16)
    own = exchange(spread(total, "z"), "z")
    margin = jnp.concatenate([own[0, part:]] * (MARGIN // 8), axis=0)
    own = jnp.concatenate([own[:, :part].reshape(block, hidden), margin], axis=0)
    return lax.all_gather(after(own, meanwhile), NEAR, axis=0, tiled=True)


def scaled_kernel(
    scale,
    full_any,
    self_any,
    neigh_any,
    bias_ref,
    full_ref,
    self_ref,
    neigh_ref,
    in_sems,
    out_sems,
):
    near, tall, _ = full_ref.shape
    half = near // 2
    block = tall - MARGIN
    order = [b for pair in zip(range(half), range(half, near)) for b in pair]
    loads, sends = {}, []
    for b in order:
        loads[b] = pltpu.make_async_copy(full_any.at[b], full_ref.at[b], in_sems.at[b])
        loads[b].start()
    for b in order:
        loads[b].wait()
        target, held = (self_any, self_ref) if b < half else (neigh_any, neigh_ref)
        here = slice(b % half * block, (b % half + 1) * block)
        held[here, :] = full_ref[b, :block, :].astype(f32) * scale
        copy = pltpu.make_async_copy(held.at[here], target.at[here], out_sems.at[b])
        copy.start()
        sends.append(copy)
    bias_ref[...] = full_ref[0, block:, :].astype(f32)[0:1] * scale
    for copy in sends:
        copy.wait()


def scaled_parts(full, width, scale):
    hidden = full.shape[1]
    near = lax.axis_size(NEAR)
    full = full.reshape(near, -1, hidden)
    grad = jax.ShapeDtypeStruct((width, hidden), f32)
    hbm = pl.BlockSpec(memory_space=pltpu.HBM)
    return pl.pallas_call(
        functools.partial(scaled_kernel, scale),
        in_specs=[hbm],
        out_specs=[hbm, hbm, pl.BlockSpec(memory_space=pltpu.VMEM)],
        out_shape=[grad, grad, jax.ShapeDtypeStruct((1, hidden), f32)],
        scratch_shapes=[
            pltpu.VMEM(full.shape, bf16),
            pltpu.VMEM(grad.shape, f32),
            pltpu.VMEM(grad.shape, f32),
            pltpu.SemaphoreType.DMA((near,)),
            pltpu.SemaphoreType.DMA((near,)),
        ],
        compiler_params=VMEM,
        cost_estimate=cost(full.size, 6 * full.size),
    )(full)


def scatter_kernel(
    turned_any, grad_any, out_ref, token_ref, turned_ref, grad_ref, sems
):
    width = out_ref.shape[1]
    copies = []
    for j in range(SPLIT):
        columns = slice(j * width, (j + 1) * width)
        for k, (source, target) in enumerate(
            (
                (turned_any.at[j], turned_ref.at[j]),
                (grad_any.at[:, columns], grad_ref.at[:, columns]),
            )
        ):
            copy = pltpu.make_async_copy(source, target, sems.at[j, k])
            copy.start()
            copies.append(copy)
    total = jnp.zeros(out_ref.shape, f32)
    for j in range(SPLIT):
        copies[2 * j].wait()
        copies[2 * j + 1].wait()
        total += jnp.dot(
            turned_ref[j],
            grad_ref[:, j * width : (j + 1) * width],
            preferred_element_type=f32,
        )
    out_ref[...] = total.astype(bf16)
    token_ref[...] = jnp.zeros(token_ref.shape, f32)


def scatter_sum(turned, slot_grad):
    _, rows, sent = turned.shape
    width = slot_grad.shape[1] // SPLIT
    return pl.pallas_call(
        scatter_kernel,
        in_specs=[pl.BlockSpec(memory_space=pltpu.HBM)] * 2,
        out_shape=[
            jax.ShapeDtypeStruct((rows, width), bf16),
            jax.ShapeDtypeStruct((8, EXTRA), f32),
        ],
        scratch_shapes=[
            pltpu.VMEM(turned.shape, bf16),
            pltpu.VMEM(slot_grad.shape, bf16),
            pltpu.SemaphoreType.DMA((SPLIT, 2)),
        ],
        compiler_params=VMEM,
        cost_estimate=cost(
            2 * SPLIT * sent * rows * width, 2 * (turned.size + slot_grad.size)
        ),
    )(turned, slot_grad)


def on_device(
    feats, seed_rows, edge_rows, edge_slots, slot_seeds, w_self, w_neigh, bias, cotangent
):
    edge_rows = edge_rows[0]
    edge_slots = edge_slots[0]
    slot_seeds = slot_seeds[0]
    sources, slot_cap = slot_seeds.shape
    s_count = slot_cap // SPLIT
    seed_count = seed_rows.shape[0]
    width = feats.shape[1]
    replicas = lax.axis_size("rep")
    select, partial_value = select_and_sum(feats, edge_rows, edge_slots, slot_cap)
    arrived = exchange(partial_value.reshape(sources, s_count, -1), DOM)
    seeds = slot_seeds.reshape(sources, SPLIT, s_count).transpose(1, 0, 2)
    seeds = seeds.reshape(SPLIT, 1, sources * s_count)
    self_rows = jnp.take(feats, seed_rows, axis=0)
    base = jnp.dot(self_rows, w_self, preferred_element_type=f32) + bias[None, :]
    hidden_out, delta, routed, terms = middle(
        arrived.reshape(sources * s_count, -1),
        seeds,
        base,
        w_neigh,
        cotangent,
        (seeds.reshape(SPLIT, -1, 1) == jnp.arange(seed_count)).astype(bf16),
        self_rows.T,
    )

    slot_grad = exchange(routed.reshape(sources, s_count, -1), DOM)
    self_grad = contract_last(delta, w_self).astype(bf16)
    local, summed = scatter_sum(
        jnp.swapaxes(select, 1, 2), slot_grad.reshape(sources * s_count, -1)
    )
    feat_grads = lax.psum_scatter(local, "rep", scatter_dimension=0, tiled=True)
    full = reduce_everywhere(terms, summed, feat_grads)
    scale = float(seed_count * lax.axis_size(DOM) * replicas) ** (-0.5)
    grad_self, grad_neigh, grad_bias = scaled_parts(full, width, scale)
    return (
        hidden_out,
        self_grad,
        feat_grads,
        grad_self,
        grad_neigh,
        grad_bias.reshape(-1),
    )


def solution(mesh):
    fine = Mesh(
        np.asarray(mesh.devices).reshape(8, 4, 2, 4), ("z", "x", "c", "rep")
    )
    every = DOM + ("rep",)
    in_specs = (
        P(DOM, None),
        P(every),
        P(every, None, None),
        P(every, None, None),
        P(every, None, None),
        P(),
        P(),
        P(),
        P(every, None),
    )
    out_specs = (P(every, None), P(every, None), P(every, None), P(), P(), P())
    return jax.shard_map(
        on_device, mesh=fine, in_specs=in_specs, out_specs=out_specs, check_vma=False
    )
```

```python
import functools

import jax
import jax.numpy as jnp
import numpy as np
from jax import lax
from jax.experimental import pallas as pl
from jax.experimental.pallas import tpu as pltpu
from jax.sharding import Mesh, PartitionSpec as P

DOM = ("z", "x", "c")
NEAR = ("c", "rep")
FAR = ("x", "z")
bf16 = jnp.bfloat16
f32 = jnp.float32

GROUP = 4
STEP = 4
SPLIT = 4
EXTRA = 128
VMEM = pltpu.CompilerParams(vmem_limit_bytes=60 * 1024 * 1024)
MARGIN = 16


def contract_first(left, right):
    return lax.dot_general(
        left, right, (((0,), (0,)), ((), ())), preferred_element_type=f32
    )


def contract_last(left, right):
    return lax.dot_general(
        left, right, (((1,), (1,)), ((), ())), preferred_element_type=f32
    )


def exchange(value, axes):
    return lax.all_to_all(value, axes, split_axis=0, concat_axis=0, tiled=True)


def spread(value, axes):
    return jnp.broadcast_to(value[None], (lax.axis_size(axes),) + value.shape)


def cost(flops, bytes_accessed):
    return pl.CostEstimate(flops=flops, bytes_accessed=bytes_accessed, transcendentals=0)


def select_kernel(rows_ref, slots_ref, feats_ref, select_ref, partial_ref):
    row_count, width = feats_ref.shape
    dests, entry_cap = rows_ref.shape
    entries = GROUP * entry_cap
    part = select_ref.shape[1] // STEP
    s_count = part // GROUP
    slots = SPLIT * part
    named = slots_ref[...]
    place = lax.broadcasted_iota(jnp.int32, named.shape, 0) % GROUP * s_count
    keys = named // s_count * part + place + named % s_count
    keys = jnp.where(named < SPLIT * s_count, keys, -1)
    row_ids = lax.broadcasted_iota(jnp.int32, (row_count, entries), 0)
    slot_ids = lax.broadcasted_iota(jnp.int32, (slots, entries), 0)
    lanes = lax.broadcasted_iota(jnp.int32, (part, EXTRA), 1)

    def side_by_side(values, step):
        first = step * GROUP
        return jnp.concatenate(
            [values[first + i : first + i + 1] for i in range(GROUP)], axis=1
        )

    for step in range(STEP):
        here = slice(step * part, (step + 1) * part)
        by_row = jnp.where(row_ids == side_by_side(rows_ref[...], step), 1.0, 0.0)
        hits = jnp.where(slot_ids == side_by_side(keys, step), 1.0, 0.0)
        chosen = contract_last(hits.astype(bf16), by_row.astype(bf16)).astype(bf16)
        count = jnp.sum(hits, axis=1, keepdims=True)
        tail = jnp.zeros((part, EXTRA), f32)
        for j in range(SPLIT):
            select_ref[j, here, :] = chosen[j * part : (j + 1) * part]
            tail = jnp.where(lanes == j, count[j * part : (j + 1) * part], tail)
        partial_ref[here, SPLIT * width :] = tail.astype(bf16)
    height = STEP * part
    chosen = select_ref[...].reshape(SPLIT * height, row_count)
    sums = jnp.dot(chosen, feats_ref[...], preferred_element_type=f32).astype(bf16)
    for j in range(SPLIT):
        partial_ref[:, j * width : (j + 1) * width] = sums[j * height : (j + 1) * height]


def select_and_sum(feats, edge_rows, edge_slots, slot_cap):
    dests, entry_cap = edge_rows.shape
    row_count, width = feats.shape
    s_count = slot_cap // SPLIT
    sent = dests * s_count
    steps = dests // (GROUP * STEP)
    wide = SPLIT * width + EXTRA
    edge_spec = pl.BlockSpec((GROUP * STEP, entry_cap), lambda i: (i, 0))
    return pl.pallas_call(
        select_kernel,
        grid=(steps,),
        in_specs=[
            edge_spec,
            edge_spec,
            pl.BlockSpec((row_count, width), lambda i: (0, 0)),
        ],
        out_specs=[
            pl.BlockSpec((SPLIT, sent // steps, row_count), lambda i: (0, i, 0)),
            pl.BlockSpec((sent // steps, wide), lambda i: (i, 0)),
        ],
        out_shape=[
            jax.ShapeDtypeStruct((SPLIT, sent, row_count), bf16),
            jax.ShapeDtypeStruct((sent, wide), bf16),
        ],
        compiler_params=VMEM,
        cost_estimate=cost(
            2 * SPLIT * sent * row_count * (width + GROUP * entry_cap),
            2 * (row_count * width + sent * (SPLIT * row_count + wide)),
        ),
    )(edge_rows, edge_slots, feats)


def middle_kernel(
    arrived_any,
    seeds_ref,
    base_any,
    w_neigh_any,
    cotangent_any,
    turned_any,
    self_any,
    hidden_any,
    delta_any,
    routed_any,
    terms_any,
    arrived_ref,
    base_ref,
    w_neigh_ref,
    cotangent_ref,
    turned_ref,
    self_ref,
    hidden_ref,
    delta_ref,
    routed_ref,
    terms_ref,
    aggregate_ref,
    neigh_ref,
    degree_ref,
    in_sems,
    out_sems,
):
    seed_count = base_ref.shape[0]
    width = w_neigh_ref.shape[0]
    sent = seeds_ref.shape[2]
    near, tall, hidden = terms_ref.shape
    block = tall - MARGIN
    ids = lax.broadcasted_iota(jnp.int32, (seed_count, sent), 0)
    lanes = lax.broadcasted_iota(jnp.int32, (seed_count, EXTRA), 1)

    def columns(j):
        return slice(j * width, (j + 1) * width if j < SPLIT else j * width + EXTRA)

    loads = []

    def load(source, target):
        copy = pltpu.make_async_copy(source, target, in_sems.at[len(loads)])
        copy.start()
        loads.append(copy)

    for j in (SPLIT, *range(SPLIT)):
        load(arrived_any.at[:, columns(j)], arrived_ref.at[:, columns(j)])

    total = jnp.zeros((seed_count, width), f32)
    counts = jnp.zeros((seed_count, EXTRA), f32)
    loads[0].wait()
    for j in range(SPLIT):
        route = jnp.where(ids == seeds_ref[j], 1.0, 0.0).astype(bf16)
        loads[1 + j].wait()
        if j == 1:
            load(w_neigh_any, w_neigh_ref)
            load(base_any, base_ref)
        if j == SPLIT - 1:
            load(cotangent_any, cotangent_ref)
            load(turned_any, turned_ref)
            load(self_any, self_ref)
        total += jnp.dot(route, arrived_ref[:, columns(j)], preferred_element_type=f32)
        found = jnp.dot(
            route, arrived_ref[:, columns(SPLIT)], preferred_element_type=f32
        )
        counts += jnp.where(lanes == j, found, 0.0)
    degree = jnp.maximum(jnp.sum(counts, axis=1, keepdims=True), 1.0)
    degree_ref[...] = jnp.broadcast_to(degree, (seed_count, EXTRA))
    aggregate_ref[...] = (total / degree).astype(bf16)
    w_neigh_load, base_load, cotangent_load, turned_load, self_load = loads[1 + SPLIT :]
    w_neigh_load.wait()
    base_load.wait()
    base_ref[...] += jnp.dot(
        aggregate_ref[...], w_neigh_ref[...], preferred_element_type=f32
    )

    cotangent_load.wait()
    rows = 16
    slope = (2.0 / np.pi) ** 0.5

    @pl.loop(0, seed_count // rows)
    def _(i):
        here = pl.ds(pl.multiple_of(i * rows, rows), rows)
        pre = base_ref[here, :]
        square = pre * pre
        bend = jnp.tanh(slope * pre * (1.0 + 0.044715 * square))
        half = 0.5 * (1.0 + bend)
        hidden_ref[here, :] = (pre * half).astype(bf16)
        steep = half + 0.5 * pre * (1.0 - bend * bend) * (
            slope * (1.0 + 3 * 0.044715 * square)
        )
        delta = (cotangent_ref[here, :].astype(f32) * steep).astype(bf16)
        delta_ref[here, :] = delta
        neigh_ref[here, :] = (delta.astype(f32) / degree_ref[here, 0:1]).astype(bf16)

    copies = []

    def send(source, target):
        copy = pltpu.make_async_copy(source, target, out_sems.at[len(copies)])
        copy.start()
        copies.append(copy)

    send(hidden_ref, hidden_any)
    send(delta_ref, delta_any)
    grad = contract_last(neigh_ref[...], w_neigh_ref[...]).astype(bf16)
    turned_load.wait()
    for j in range(SPLIT):
        routed_ref[:, columns(j)] = jnp.dot(
            turned_ref[j], grad, preferred_element_type=f32
        ).astype(bf16)
        send(routed_ref.at[:, columns(j)], routed_any.at[:, columns(j)])

    self_load.wait()
    delta = delta_ref[...]
    column = jnp.sum(delta.astype(f32), axis=0, keepdims=True)
    first = lax.broadcasted_iota(jnp.int32, (MARGIN, hidden), 0) == 0
    margin = jnp.where(first, column, 0.0).astype(bf16)
    half = near // 2
    products = (
        jnp.dot(self_ref[...], delta, preferred_element_type=f32),
        contract_first(aggregate_ref[...], delta),
    )
    for side, product in enumerate(products):
        product = product.astype(bf16)
        mine = slice(side * half, (side + 1) * half)
        for b in range(half):
            terms_ref[side * half + b, :block, :] = product[b * block : (b + 1) * block]
            terms_ref[side * half + b, block:, :] = margin
        send(terms_ref.at[mine], terms_any.at[mine])
    for copy in copies:
        copy.wait()


def middle(arrived, seeds, base, w_neigh, cotangent, turned, self_turned):
    sent, wide = arrived.shape
    seed_count, hidden = base.shape
    width = w_neigh.shape[0]
    near = lax.axis_size(NEAR)
    terms = (near, 2 * width // near + MARGIN, hidden)
    hbm = pl.BlockSpec(memory_space=pltpu.HBM)
    loaded = (arrived, base, w_neigh, cotangent, turned, self_turned)
    results = [
        jax.ShapeDtypeStruct((seed_count, hidden), bf16),
        jax.ShapeDtypeStruct((seed_count, hidden), bf16),
        jax.ShapeDtypeStruct((sent, SPLIT * width), bf16),
        jax.ShapeDtypeStruct(terms, bf16),
    ]
    return pl.pallas_call(
        middle_kernel,
        in_specs=[hbm, pl.BlockSpec(memory_space=pltpu.VMEM)] + [hbm] * 5,
        out_specs=[hbm] * 4,
        out_shape=results,
        scratch_shapes=[pltpu.VMEM(one.shape, one.dtype) for one in (*loaded, *results)]
        + [
            pltpu.VMEM((seed_count, width), bf16),
            pltpu.VMEM((seed_count, hidden), bf16),
            pltpu.VMEM((seed_count, EXTRA), f32),
            pltpu.SemaphoreType.DMA((SPLIT + 6,)),
            pltpu.SemaphoreType.DMA((SPLIT + 4,)),
        ],
        compiler_params=VMEM,
        cost_estimate=cost(
            4 * seed_count * width * (SPLIT * sent + 2 * hidden),
            2 * (2 * arrived.size + 3 * w_neigh.size + 5 * base.size),
        ),
    )(arrived, seeds, base, w_neigh, cotangent, turned, self_turned)


def after(value, earlier):
    def kernel(value_ref, earlier_ref, out_ref):
        pass

    return pl.pallas_call(
        kernel,
        in_specs=[pl.BlockSpec(memory_space=pl.ANY)] * 2,
        out_specs=pl.BlockSpec(memory_space=pl.ANY),
        out_shape=jax.ShapeDtypeStruct(value.shape, value.dtype),
        input_output_aliases={0: 0},
    )(value, earlier)


def reduce_everywhere(terms, earlier, meanwhile):
    _, tall, hidden = terms.shape
    block = tall - MARGIN
    part = block // lax.axis_size("x")
    summed = lax.psum_scatter(
        terms.reshape(-1, hidden), NEAR, scatter_dimension=0, tiled=True
    )
    parts = summed[:block].reshape(-1, part, hidden)
    margin = jnp.broadcast_to(summed[None, block:], (block // part, MARGIN, hidden))
    parts = jnp.concatenate([parts, margin], axis=1)
    line = lax.psum_scatter(
        parts.reshape(-1, hidden), "x", scatter_dimension=0, tiled=True
    )
    pieces = after(line, earlier).reshape(lax.axis_size("z"), -1, hidden)
    total = jnp.sum(exchange(pieces, "z").astype(f32), axis=0).astype(bf16)
    own = exchange(spread(total, FAR), FAR).reshape(-1, part + MARGIN, hidden)
    own = jnp.concatenate([own[:, :part].reshape(block, hidden), own[0, part:]], axis=0)
    return lax.all_gather(after(own, meanwhile), NEAR, axis=0, tiled=True)


def scaled_kernel(
    scale,
    full_any,
    self_any,
    neigh_any,
    bias_ref,
    full_ref,
    self_ref,
    neigh_ref,
    in_sems,
    out_sems,
):
    near, tall, _ = full_ref.shape
    half = near // 2
    block = tall - MARGIN
    order = [b for pair in zip(range(half), range(half, near)) for b in pair]
    loads, sends = {}, []
    for b in order:
        loads[b] = pltpu.make_async_copy(full_any.at[b], full_ref.at[b], in_sems.at[b])
        loads[b].start()
    for b in order:
        loads[b].wait()
        target, held = (self_any, self_ref) if b < half else (neigh_any, neigh_ref)
        here = slice(b % half * block, (b % half + 1) * block)
        held[here, :] = full_ref[b, :block, :].astype(f32) * scale
        copy = pltpu.make_async_copy(held.at[here], target.at[here], out_sems.at[b])
        copy.start()
        sends.append(copy)
    bias_ref[...] = full_ref[0, block:, :].astype(f32)[0:1] * scale
    for copy in sends:
        copy.wait()


def scaled_parts(full, width, scale):
    hidden = full.shape[1]
    near = lax.axis_size(NEAR)
    full = full.reshape(near, -1, hidden)
    grad = jax.ShapeDtypeStruct((width, hidden), f32)
    hbm = pl.BlockSpec(memory_space=pltpu.HBM)
    return pl.pallas_call(
        functools.partial(scaled_kernel, scale),
        in_specs=[hbm],
        out_specs=[hbm, hbm, pl.BlockSpec(memory_space=pltpu.VMEM)],
        out_shape=[grad, grad, jax.ShapeDtypeStruct((1, hidden), f32)],
        scratch_shapes=[
            pltpu.VMEM(full.shape, bf16),
            pltpu.VMEM(grad.shape, f32),
            pltpu.VMEM(grad.shape, f32),
            pltpu.SemaphoreType.DMA((near,)),
            pltpu.SemaphoreType.DMA((near,)),
        ],
        compiler_params=VMEM,
        cost_estimate=cost(full.size, 6 * full.size),
    )(full)


def scatter_kernel(turned_ref, grad_ref, out_ref, token_ref):
    width = out_ref.shape[1]
    total = jnp.zeros(out_ref.shape, f32)
    for j in range(SPLIT):
        total += jnp.dot(
            turned_ref[j],
            grad_ref[:, j * width : (j + 1) * width],
            preferred_element_type=f32,
        )
    out_ref[...] = total.astype(bf16)
    token_ref[...] = jnp.zeros(token_ref.shape, f32)


def scatter_sum(turned, slot_grad):
    _, rows, sent = turned.shape
    width = slot_grad.shape[1] // SPLIT
    steps = 2
    tall = rows // steps
    return pl.pallas_call(
        scatter_kernel,
        grid=(steps,),
        in_specs=[
            pl.BlockSpec((SPLIT, tall, sent), lambda i: (0, i, 0)),
            pl.BlockSpec(slot_grad.shape, lambda i: (0, 0)),
        ],
        out_specs=[
            pl.BlockSpec((tall, width), lambda i: (i, 0)),
            pl.BlockSpec((8, EXTRA), lambda i: (0, 0)),
        ],
        out_shape=[
            jax.ShapeDtypeStruct((rows, width), bf16),
            jax.ShapeDtypeStruct((8, EXTRA), f32),
        ],
        compiler_params=VMEM,
        cost_estimate=cost(
            2 * SPLIT * sent * rows * width, 2 * (turned.size + slot_grad.size)
        ),
    )(turned, slot_grad)


def on_device(
    feats, seed_rows, edge_rows, edge_slots, slot_seeds, w_self, w_neigh, bias, cotangent
):
    edge_rows = edge_rows[0]
    edge_slots = edge_slots[0]
    slot_seeds = slot_seeds[0]
    sources, slot_cap = slot_seeds.shape
    s_count = slot_cap // SPLIT
    seed_count = seed_rows.shape[0]
    width = feats.shape[1]
    replicas = lax.axis_size("rep")
    select, partial_value = select_and_sum(feats, edge_rows, edge_slots, slot_cap)
    arrived = exchange(partial_value.reshape(sources, s_count, -1), DOM)
    seeds = slot_seeds.reshape(sources, SPLIT, s_count).transpose(1, 0, 2)
    seeds = seeds.reshape(SPLIT, 1, sources * s_count)
    self_rows = jnp.take(feats, seed_rows, axis=0)
    base = jnp.dot(self_rows, w_self, preferred_element_type=f32) + bias[None, :]
    hidden_out, delta, routed, terms = middle(
        arrived.reshape(sources * s_count, -1),
        seeds,
        base,
        w_neigh,
        cotangent,
        (seeds.reshape(SPLIT, -1, 1) == jnp.arange(seed_count)).astype(bf16),
        self_rows.T,
    )

    slot_grad = exchange(routed.reshape(sources, s_count, -1), DOM)
    self_grad = contract_last(delta, w_self).astype(bf16)
    local, summed = scatter_sum(
        jnp.swapaxes(select, 1, 2), slot_grad.reshape(sources * s_count, -1)
    )
    feat_grads = lax.psum_scatter(local, "rep", scatter_dimension=0, tiled=True)
    full = reduce_everywhere(terms, summed, feat_grads)
    scale = float(seed_count * lax.axis_size(DOM) * replicas) ** (-0.5)
    grad_self, grad_neigh, grad_bias = scaled_parts(full, width, scale)
    return (
        hidden_out,
        self_grad,
        feat_grads,
        grad_self,
        grad_neigh,
        grad_bias.reshape(-1),
    )


def solution(mesh):
    fine = Mesh(
        np.asarray(mesh.devices).reshape(8, 4, 2, 4), ("z", "x", "c", "rep")
    )
    every = DOM + ("rep",)
    in_specs = (
        P(DOM, None),
        P(every),
        P(every, None, None),
        P(every, None, None),
        P(every, None, None),
        P(),
        P(),
        P(),
        P(every, None),
    )
    out_specs = (P(every, None), P(every, None), P(every, None), P(), P(), P())
    return jax.shard_map(
        on_device, mesh=fine, in_specs=in_specs, out_specs=out_specs, check_vma=False
    )
```

```python
import functools

import jax
import jax.numpy as jnp
import numpy as np
from jax import lax
from jax.experimental import pallas as pl
from jax.experimental.pallas import tpu as pltpu
from jax.sharding import Mesh, PartitionSpec as P

DOM = ("z", "x", "c")
NEAR = ("c", "rep")
FAR = ("x", "z")
bf16 = jnp.bfloat16
f32 = jnp.float32

GROUP = 4
STEP = 2
SPLIT = 4
EXTRA = 128
VMEM = pltpu.CompilerParams(vmem_limit_bytes=60 * 1024 * 1024)
MARGIN = 16


def contract_first(left, right):
    return lax.dot_general(
        left, right, (((0,), (0,)), ((), ())), preferred_element_type=f32
    )


def contract_last(left, right):
    return lax.dot_general(
        left, right, (((1,), (1,)), ((), ())), preferred_element_type=f32
    )


def exchange(value, axes):
    return lax.all_to_all(value, axes, split_axis=0, concat_axis=0, tiled=True)


def spread(value, axes):
    return jnp.broadcast_to(value[None], (lax.axis_size(axes),) + value.shape)


def cost(flops, bytes_accessed):
    return pl.CostEstimate(flops=flops, bytes_accessed=bytes_accessed, transcendentals=0)


def select_kernel(rows_ref, slots_ref, feats_ref, select_ref, partial_ref):
    row_count, width = feats_ref.shape
    dests, entry_cap = rows_ref.shape
    entries = GROUP * entry_cap
    part = select_ref.shape[1] // STEP
    s_count = part // GROUP
    slots = SPLIT * part
    named = slots_ref[...]
    place = lax.broadcasted_iota(jnp.int32, named.shape, 0) % GROUP * s_count
    keys = named // s_count * part + place + named % s_count
    keys = jnp.where(named < SPLIT * s_count, keys, -1)
    row_ids = lax.broadcasted_iota(jnp.int32, (row_count, entries), 0)
    slot_ids = lax.broadcasted_iota(jnp.int32, (slots, entries), 0)
    lanes = lax.broadcasted_iota(jnp.int32, (part, EXTRA), 1)

    def side_by_side(values, step):
        first = step * GROUP
        return jnp.concatenate(
            [values[first + i : first + i + 1] for i in range(GROUP)], axis=1
        )

    for step in range(STEP):
        here = slice(step * part, (step + 1) * part)
        by_row = jnp.where(row_ids == side_by_side(rows_ref[...], step), 1.0, 0.0)
        hits = jnp.where(slot_ids == side_by_side(keys, step), 1.0, 0.0)
        chosen = contract_last(hits.astype(bf16), by_row.astype(bf16)).astype(bf16)
        count = jnp.sum(hits, axis=1, keepdims=True)
        tail = jnp.zeros((part, EXTRA), f32)
        for j in range(SPLIT):
            select_ref[j, here, :] = chosen[j * part : (j + 1) * part]
            tail = jnp.where(lanes == j, count[j * part : (j + 1) * part], tail)
        partial_ref[here, SPLIT * width :] = tail.astype(bf16)
    height = STEP * part
    chosen = select_ref[...].reshape(SPLIT * height, row_count)
    sums = jnp.dot(chosen, feats_ref[...], preferred_element_type=f32).astype(bf16)
    for j in range(SPLIT):
        partial_ref[:, j * width : (j + 1) * width] = sums[j * height : (j + 1) * height]


def select_and_sum(feats, edge_rows, edge_slots, slot_cap):
    dests, entry_cap = edge_rows.shape
    row_count, width = feats.shape
    s_count = slot_cap // SPLIT
    sent = dests * s_count
    steps = dests // (GROUP * STEP)
    wide = SPLIT * width + EXTRA
    edge_spec = pl.BlockSpec((GROUP * STEP, entry_cap), lambda i: (i, 0))
    return pl.pallas_call(
        select_kernel,
        grid=(steps,),
        in_specs=[
            edge_spec,
            edge_spec,
            pl.BlockSpec((row_count, width), lambda i: (0, 0)),
        ],
        out_specs=[
            pl.BlockSpec((SPLIT, sent // steps, row_count), lambda i: (0, i, 0)),
            pl.BlockSpec((sent // steps, wide), lambda i: (i, 0)),
        ],
        out_shape=[
            jax.ShapeDtypeStruct((SPLIT, sent, row_count), bf16),
            jax.ShapeDtypeStruct((sent, wide), bf16),
        ],
        compiler_params=VMEM,
        cost_estimate=cost(
            2 * SPLIT * sent * row_count * (width + GROUP * entry_cap),
            2 * (row_count * width + sent * (SPLIT * row_count + wide)),
        ),
    )(edge_rows, edge_slots, feats)


def middle_kernel(
    arrived_any,
    seeds_ref,
    base_any,
    w_neigh_any,
    cotangent_any,
    turned_any,
    self_any,
    hidden_any,
    delta_any,
    routed_any,
    terms_any,
    arrived_ref,
    base_ref,
    w_neigh_ref,
    cotangent_ref,
    turned_ref,
    self_ref,
    hidden_ref,
    delta_ref,
    routed_ref,
    terms_ref,
    aggregate_ref,
    neigh_ref,
    degree_ref,
    in_sems,
    out_sems,
):
    seed_count = base_ref.shape[0]
    width = w_neigh_ref.shape[0]
    sent = seeds_ref.shape[2]
    near, tall, hidden = terms_ref.shape
    block = tall - MARGIN
    ids = lax.broadcasted_iota(jnp.int32, (seed_count, sent), 0)
    lanes = lax.broadcasted_iota(jnp.int32, (seed_count, EXTRA), 1)

    def columns(j):
        return slice(j * width, (j + 1) * width if j < SPLIT else j * width + EXTRA)

    loads = []

    def load(source, target):
        copy = pltpu.make_async_copy(source, target, in_sems.at[len(loads)])
        copy.start()
        loads.append(copy)

    for j in (SPLIT, *range(SPLIT)):
        load(arrived_any.at[:, columns(j)], arrived_ref.at[:, columns(j)])

    total = jnp.zeros((seed_count, width), f32)
    counts = jnp.zeros((seed_count, EXTRA), f32)
    loads[0].wait()
    for j in range(SPLIT):
        route = jnp.where(ids == seeds_ref[j], 1.0, 0.0).astype(bf16)
        loads[1 + j].wait()
        if j == 1:
            load(w_neigh_any, w_neigh_ref)
            load(base_any, base_ref)
        if j == SPLIT - 1:
            load(cotangent_any, cotangent_ref)
            load(turned_any, turned_ref)
            load(self_any, self_ref)
        total += jnp.dot(route, arrived_ref[:, columns(j)], preferred_element_type=f32)
        found = jnp.dot(
            route, arrived_ref[:, columns(SPLIT)], preferred_element_type=f32
        )
        counts += jnp.where(lanes == j, found, 0.0)
    degree = jnp.maximum(jnp.sum(counts, axis=1, keepdims=True), 1.0)
    degree_ref[...] = jnp.broadcast_to(degree, (seed_count, EXTRA))
    aggregate_ref[...] = (total / degree).astype(bf16)
    w_neigh_load, base_load, cotangent_load, turned_load, self_load = loads[1 + SPLIT :]
    w_neigh_load.wait()
    base_load.wait()
    base_ref[...] += jnp.dot(
        aggregate_ref[...], w_neigh_ref[...], preferred_element_type=f32
    )

    cotangent_load.wait()
    rows = 16
    slope = (2.0 / np.pi) ** 0.5

    @pl.loop(0, seed_count // rows)
    def _(i):
        here = pl.ds(pl.multiple_of(i * rows, rows), rows)
        pre = base_ref[here, :]
        square = pre * pre
        bend = jnp.tanh(slope * pre * (1.0 + 0.044715 * square))
        half = 0.5 * (1.0 + bend)
        hidden_ref[here, :] = (pre * half).astype(bf16)
        steep = half + 0.5 * pre * (1.0 - bend * bend) * (
            slope * (1.0 + 3 * 0.044715 * square)
        )
        delta = (cotangent_ref[here, :].astype(f32) * steep).astype(bf16)
        delta_ref[here, :] = delta
        neigh_ref[here, :] = (delta.astype(f32) / degree_ref[here, 0:1]).astype(bf16)

    copies = []

    def send(source, target):
        copy = pltpu.make_async_copy(source, target, out_sems.at[len(copies)])
        copy.start()
        copies.append(copy)

    send(hidden_ref, hidden_any)
    send(delta_ref, delta_any)
    grad = contract_last(neigh_ref[...], w_neigh_ref[...]).astype(bf16)
    turned_load.wait()
    for j in range(SPLIT):
        routed_ref[:, columns(j)] = jnp.dot(
            turned_ref[j], grad, preferred_element_type=f32
        ).astype(bf16)
        send(routed_ref.at[:, columns(j)], routed_any.at[:, columns(j)])

    self_load.wait()
    delta = delta_ref[...]
    column = jnp.sum(delta.astype(f32), axis=0, keepdims=True)
    first = lax.broadcasted_iota(jnp.int32, (MARGIN, hidden), 0) == 0
    margin = jnp.where(first, column, 0.0).astype(bf16)
    half = near // 2
    products = (
        jnp.dot(self_ref[...], delta, preferred_element_type=f32),
        contract_first(aggregate_ref[...], delta),
    )
    for side, product in enumerate(products):
        product = product.astype(bf16)
        mine = slice(side * half, (side + 1) * half)
        for b in range(half):
            terms_ref[side * half + b, :block, :] = product[b * block : (b + 1) * block]
            terms_ref[side * half + b, block:, :] = margin
        send(terms_ref.at[mine], terms_any.at[mine])
    for copy in copies:
        copy.wait()


def middle(arrived, seeds, base, w_neigh, cotangent, turned, self_turned):
    sent, wide = arrived.shape
    seed_count, hidden = base.shape
    width = w_neigh.shape[0]
    near = lax.axis_size(NEAR)
    terms = (near, 2 * width // near + MARGIN, hidden)
    hbm = pl.BlockSpec(memory_space=pltpu.HBM)
    loaded = (arrived, base, w_neigh, cotangent, turned, self_turned)
    results = [
        jax.ShapeDtypeStruct((seed_count, hidden), bf16),
        jax.ShapeDtypeStruct((seed_count, hidden), bf16),
        jax.ShapeDtypeStruct((sent, SPLIT * width), bf16),
        jax.ShapeDtypeStruct(terms, bf16),
    ]
    return pl.pallas_call(
        middle_kernel,
        in_specs=[hbm, pl.BlockSpec(memory_space=pltpu.VMEM)] + [hbm] * 5,
        out_specs=[hbm] * 4,
        out_shape=results,
        scratch_shapes=[pltpu.VMEM(one.shape, one.dtype) for one in (*loaded, *results)]
        + [
            pltpu.VMEM((seed_count, width), bf16),
            pltpu.VMEM((seed_count, hidden), bf16),
            pltpu.VMEM((seed_count, EXTRA), f32),
            pltpu.SemaphoreType.DMA((SPLIT + 6,)),
            pltpu.SemaphoreType.DMA((SPLIT + 4,)),
        ],
        compiler_params=VMEM,
        cost_estimate=cost(
            4 * seed_count * width * (SPLIT * sent + 2 * hidden),
            2 * (2 * arrived.size + 3 * w_neigh.size + 5 * base.size),
        ),
    )(arrived, seeds, base, w_neigh, cotangent, turned, self_turned)


def after(value, earlier):
    def kernel(value_ref, earlier_ref, out_ref):
        pass

    return pl.pallas_call(
        kernel,
        in_specs=[pl.BlockSpec(memory_space=pl.ANY)] * 2,
        out_specs=pl.BlockSpec(memory_space=pl.ANY),
        out_shape=jax.ShapeDtypeStruct(value.shape, value.dtype),
        input_output_aliases={0: 0},
    )(value, earlier)


def reduce_everywhere(terms, earlier, meanwhile):
    _, tall, hidden = terms.shape
    block = tall - MARGIN
    part = block // lax.axis_size("x")
    summed = lax.psum_scatter(
        terms.reshape(-1, hidden), NEAR, scatter_dimension=0, tiled=True
    )
    parts = summed[:block].reshape(-1, part, hidden)
    margin = jnp.broadcast_to(summed[None, block:], (block // part, MARGIN, hidden))
    parts = jnp.concatenate([parts, margin], axis=1)
    line = lax.psum_scatter(
        parts.reshape(-1, hidden), "x", scatter_dimension=0, tiled=True
    )
    pieces = after(line, earlier).reshape(lax.axis_size("z"), -1, hidden)
    total = jnp.sum(exchange(pieces, "z").astype(f32), axis=0).astype(bf16)
    own = exchange(spread(total, FAR), FAR).reshape(-1, part + MARGIN, hidden)
    own = jnp.concatenate([own[:, :part].reshape(block, hidden), own[0, part:]], axis=0)
    return lax.all_gather(after(own, meanwhile), NEAR, axis=0, tiled=True)


def scaled_kernel(
    scale,
    full_any,
    self_any,
    neigh_any,
    bias_ref,
    full_ref,
    self_ref,
    neigh_ref,
    in_sems,
    out_sems,
):
    near, tall, _ = full_ref.shape
    half = near // 2
    block = tall - MARGIN
    order = [b for pair in zip(range(half), range(half, near)) for b in pair]
    loads, sends = {}, []
    for b in order:
        loads[b] = pltpu.make_async_copy(full_any.at[b], full_ref.at[b], in_sems.at[b])
        loads[b].start()
    for b in order:
        loads[b].wait()
        target, held = (self_any, self_ref) if b < half else (neigh_any, neigh_ref)
        here = slice(b % half * block, (b % half + 1) * block)
        held[here, :] = full_ref[b, :block, :].astype(f32) * scale
        copy = pltpu.make_async_copy(held.at[here], target.at[here], out_sems.at[b])
        copy.start()
        sends.append(copy)
    bias_ref[...] = full_ref[0, block:, :].astype(f32)[0:1] * scale
    for copy in sends:
        copy.wait()


def scaled_parts(full, width, scale):
    hidden = full.shape[1]
    near = lax.axis_size(NEAR)
    full = full.reshape(near, -1, hidden)
    grad = jax.ShapeDtypeStruct((width, hidden), f32)
    hbm = pl.BlockSpec(memory_space=pltpu.HBM)
    return pl.pallas_call(
        functools.partial(scaled_kernel, scale),
        in_specs=[hbm],
        out_specs=[hbm, hbm, pl.BlockSpec(memory_space=pltpu.VMEM)],
        out_shape=[grad, grad, jax.ShapeDtypeStruct((1, hidden), f32)],
        scratch_shapes=[
            pltpu.VMEM(full.shape, bf16),
            pltpu.VMEM(grad.shape, f32),
            pltpu.VMEM(grad.shape, f32),
            pltpu.SemaphoreType.DMA((near,)),
            pltpu.SemaphoreType.DMA((near,)),
        ],
        compiler_params=VMEM,
        cost_estimate=cost(full.size, 6 * full.size),
    )(full)


def scatter_kernel(turned_ref, grad_ref, out_ref, token_ref):
    width = out_ref.shape[1]
    total = jnp.zeros(out_ref.shape, f32)
    for j in range(SPLIT):
        total += jnp.dot(
            turned_ref[j],
            grad_ref[:, j * width : (j + 1) * width],
            preferred_element_type=f32,
        )
    out_ref[...] = total.astype(bf16)
    token_ref[...] = jnp.zeros(token_ref.shape, f32)


def scatter_sum(turned, slot_grad):
    _, rows, sent = turned.shape
    width = slot_grad.shape[1] // SPLIT
    steps = 2
    tall = rows // steps
    return pl.pallas_call(
        scatter_kernel,
        grid=(steps,),
        in_specs=[
            pl.BlockSpec((SPLIT, tall, sent), lambda i: (0, i, 0)),
            pl.BlockSpec(slot_grad.shape, lambda i: (0, 0)),
        ],
        out_specs=[
            pl.BlockSpec((tall, width), lambda i: (i, 0)),
            pl.BlockSpec((8, EXTRA), lambda i: (0, 0)),
        ],
        out_shape=[
            jax.ShapeDtypeStruct((rows, width), bf16),
            jax.ShapeDtypeStruct((8, EXTRA), f32),
        ],
        compiler_params=VMEM,
        cost_estimate=cost(
            2 * SPLIT * sent * rows * width, 2 * (turned.size + slot_grad.size)
        ),
    )(turned, slot_grad)


def on_device(
    feats, seed_rows, edge_rows, edge_slots, slot_seeds, w_self, w_neigh, bias, cotangent
):
    edge_rows = edge_rows[0]
    edge_slots = edge_slots[0]
    slot_seeds = slot_seeds[0]
    sources, slot_cap = slot_seeds.shape
    s_count = slot_cap // SPLIT
    seed_count = seed_rows.shape[0]
    width = feats.shape[1]
    replicas = lax.axis_size("rep")
    select, partial_value = select_and_sum(feats, edge_rows, edge_slots, slot_cap)
    arrived = exchange(partial_value.reshape(sources, s_count, -1), DOM)
    seeds = slot_seeds.reshape(sources, SPLIT, s_count).transpose(1, 0, 2)
    seeds = seeds.reshape(SPLIT, 1, sources * s_count)
    self_rows = jnp.take(feats, seed_rows, axis=0)
    base = jnp.dot(self_rows, w_self, preferred_element_type=f32) + bias[None, :]
    hidden_out, delta, routed, terms = middle(
        arrived.reshape(sources * s_count, -1),
        seeds,
        base,
        w_neigh,
        cotangent,
        (seeds.reshape(SPLIT, -1, 1) == jnp.arange(seed_count)).astype(bf16),
        self_rows.T,
    )

    slot_grad = exchange(routed.reshape(sources, s_count, -1), DOM)
    self_grad = contract_last(delta, w_self).astype(bf16)
    local, summed = scatter_sum(
        jnp.swapaxes(select, 1, 2), slot_grad.reshape(sources * s_count, -1)
    )
    feat_grads = lax.psum_scatter(local, "rep", scatter_dimension=0, tiled=True)
    full = reduce_everywhere(terms, summed, feat_grads)
    scale = float(seed_count * lax.axis_size(DOM) * replicas) ** (-0.5)
    grad_self, grad_neigh, grad_bias = scaled_parts(full, width, scale)
    return (
        hidden_out,
        self_grad,
        feat_grads,
        grad_self,
        grad_neigh,
        grad_bias.reshape(-1),
    )


def solution(mesh):
    fine = Mesh(
        np.asarray(mesh.devices).reshape(8, 4, 2, 4), ("z", "x", "c", "rep")
    )
    every = DOM + ("rep",)
    in_specs = (
        P(DOM, None),
        P(every),
        P(every, None, None),
        P(every, None, None),
        P(every, None, None),
        P(),
        P(),
        P(),
        P(every, None),
    )
    out_specs = (P(every, None), P(every, None), P(every, None), P(), P(), P())
    return jax.shard_map(
        on_device, mesh=fine, in_specs=in_specs, out_specs=out_specs, check_vma=False
    )
```
